32 devices in a mesh: depth: 8 (over z, y), tile: 4 (over x, core).
Axes of the slice: x: 2, y: 2, z: 4, core: 2. Of those that a mesh axis runs over, the one named last changes fastest.
Arguments:
- volume: bfloat16 [96, 4, 768, 512], P('depth', 'tile'), may hold values from -6 to 6
- table_index: int32 [96, 4, 768, 32], P('depth', 'tile'), may hold values from 0 to 15
- brick_position: int32 [8], replicated, may hold values from 0 to 7, each once
- tf_center: float32 [16], replicated, may hold values from -1.5 to 1.5
- tf_width: float32 [16], replicated, may hold values from 0.3 to 1.2
- tf_peak: float32 [16], replicated, may hold values from 2 to 32
- tf_color: float32 [3, 16], replicated, may hold values from 0.1 to 1
Outputs:
- frame: float32 [4, 4, 768, 512], P(None, 'tile', 'depth')
The draws below stay inside these ranges and needn't reach their ends.
Inputs may be any that keep to these rules, and one draw needn't show every extreme that they name: `brick_position`: each depth rank has a different position.
All inputs are finite; a program needn't handle non-finite values.
Results may differ from the reference program's by a relative error of at most 0.0003.
Values may be sent and summed in bfloat16 or wider, within the bound.
A program may use at most 128 MiB of HBM per device.

```python
import math
import jax
import jax.numpy as jnp
from jax import lax

SLAB = 12
TH = 768
TW = 512
TABLE = 16
CELL = 16
NZ = 96
CELLS = 32
N_DEPTH = 8
N_TILE = 4


def place_ends(entries, stream_key, low, largest):
    longest = entries.shape.index(max(entries.shape))
    spots = []
    for shift in (0, 1):
        where = [jax.random.randint(jax.random.fold_in(stream_key, axis), (), 0, length) for axis, length in enumerate(entries.shape)]
        where[longest] = (where[longest] + shift) % entries.shape[longest]
        spots.append(tuple(where))
    return entries.at[spots[0]].set(low).at[spots[1]].set(largest)


def shard_levels(stream_key, extent, split, low, high):
    factor_of = 1.0
    for dim, blocks in split:
        steps = jax.random.uniform(jax.random.fold_in(jax.random.fold_in(stream_key, 6), dim), (blocks,), jnp.float32, low / len(split), high / len(split))
        factor_of = factor_of * jnp.repeat(jnp.exp(steps), extent[dim] // blocks).reshape((-1,) + (1,) * (len(extent) - 1 - dim))
    return factor_of


def normal_values(stream_key, dims, deviation, reach, cuts=(), kind=jnp.bfloat16):
    values = jax.random.normal(stream_key, dims, jnp.float32) * deviation
    if len(cuts) > 0:
        values = shard_levels(stream_key, dims, cuts, -0.22, 0.18) * values
    return jnp.clip(values, min=-reach, max=reach).astype(kind)


def setup_inputs(seed: int = 0) -> dict:
    seeds = jax.random.split(jax.random.key(seed), 8)
    return {
        "volume": normal_values(seeds[0], (NZ, N_TILE, TH, TW), 1.0, 6.0, ((0, 8), (1, 4))),
        "table_index": place_ends(jax.random.randint(seeds[1], (NZ, N_TILE, TH, CELLS), 0, TABLE), jax.random.fold_in(seeds[1], 1), 0, TABLE - 1).astype(jnp.int32),
        "brick_position": jax.random.permutation(seeds[2], N_DEPTH).astype(jnp.int32),
        "tf_center": jnp.clip(jax.random.uniform(seeds[3], (TABLE,), jnp.float32, -1.5, 1.5), -1.5, 1.5),
        "tf_width": jnp.clip(jnp.exp(jax.random.uniform(seeds[4], (TABLE,), jnp.float32, math.log(0.3), math.log(1.2))), 0.3, 1.2),
        "tf_peak": jnp.clip(jnp.exp(jax.random.uniform(seeds[5], (TABLE,), jnp.float32, math.log(2.0), math.log(32.0))), 2.0, 32.0),
        "tf_color": jnp.clip(jax.random.uniform(seeds[6], (3, TABLE), jnp.float32, 0.1, 1.0), 0.1, 1.0),
    }


def light_sample(value, grad_x, grad_y, params, rgb, trans, inverse):
    energy = grad_x * grad_x + grad_y * grad_y
    facing = 0.6 * grad_x + 0.8 * grad_y
    shade = 0.3 + 0.7 * facing * facing / (1.0 + energy)
    scaled = (value - params[0]) / params[1]
    extinction = params[2] * jnp.exp(-0.5 * scaled * scaled) * energy * inverse
    keep = jnp.exp(-extinction)
    opacity = 1.0 - keep
    weight = trans * opacity
    rgb = rgb + weight[None] * params[3:6] * shade[None]
    trans = trans * keep
    return rgb, trans


def to_plane(block):
    shape = block.shape
    block = block.reshape(shape[0], 2, 2, shape[2], shape[3])
    return block.transpose(0, 1, 3, 2, 4).reshape(shape[0], 2 * shape[2], 2 * shape[3])


def march(padded, cells, tables):
    height = cells.shape[1]
    width = cells.shape[2]
    inverse = 1.0 / NZ

    def sample(step, carry):
        rgb, trans = carry
        plane = lax.dynamic_index_in_dim(padded, step, 0, keepdims=False)
        index = lax.dynamic_index_in_dim(cells, step, 0, keepdims=False)
        value = plane[1:-1, 1:-1]
        grad_x = 0.5 * (plane[1:-1, 2:] - plane[1:-1, :-2])
        grad_y = 0.5 * (plane[2:, 1:-1] - plane[:-2, 1:-1])
        params = jnp.take(tables, index, axis=1)
        return light_sample(value, grad_x, grad_y, params, rgb, trans, inverse)

    start = (jnp.zeros((3, height, width), jnp.float32), jnp.ones((height, width), jnp.float32))
    rgb, trans = lax.fori_loop(0, SLAB, sample, start)
    return jnp.concatenate([rgb, (1.0 - trans)[None]], axis=0)


def reference(volume, table_index, brick_position, tf_center, tf_width, tf_peak, tf_color):
    tables = jnp.concatenate([tf_center[None], tf_width[None], tf_peak[None], tf_color], axis=0).astype(jnp.float32)
    rank_at = jnp.argsort(brick_position).astype(jnp.int32)

    def step(image, place):
        rank = rank_at[place]
        brick = lax.dynamic_slice_in_dim(volume, rank * SLAB, SLAB, 0)
        cells = lax.dynamic_slice_in_dim(table_index, rank * SLAB, SLAB, 0)
        plane = to_plane(brick.astype(jnp.float32))
        index = to_plane(jnp.repeat(cells, CELL, axis=3))
        padded = jnp.pad(plane, ((0, 0), (1, 1), (1, 1)))
        partial_value = march(padded, index, tables)
        return image + (1.0 - image[3:4]) * partial_value, None

    start = jnp.zeros((4, 2 * TH, 2 * TW), jnp.float32)
    image, unused = lax.scan(step, start, jnp.arange(N_DEPTH, dtype=jnp.int32))
    image = image.reshape(4, 2, TH, 2, TW).transpose(0, 1, 3, 2, 4)
    return image.reshape(4, 4, TH, TW)
```

```python
import functools
import math
import jax
import jax.numpy as jnp
from jax import lax
from jax.experimental import pallas as pl
from jax.experimental.pallas import tpu as pltpu
from jax.sharding import PartitionSpec as P

CELL = 16
ROWS = 16
LANES = 128
OCTAVES = 30.0
TOP_CODE = 65535.0
MID_CODE = 32768
SCALE = TOP_CODE / OCTAVES
LOG2E = 1.0 / math.log(2.0)
PARTS = 3
MESH = pl.DeviceIdType.MESH


def encode(value):
    code = jnp.log(value) * (-SCALE * LOG2E)
    code = jnp.minimum(jnp.maximum(code, 0.0), TOP_CODE)
    return ((code + 0.5).astype(jnp.int32) - MID_CODE).astype(jnp.int16)


def decode(code):
    steps = code.astype(jnp.int32).astype(jnp.float32)
    value = jnp.exp2((steps + float(MID_CODE)) * (-1.0 / SCALE))
    return jnp.where(steps >= TOP_CODE - MID_CODE, 0.0, value)


def march_kernel(
    ranks,
    tiles,
    entries,
    position_ref,
    table_ref,
    index_ref,
    volume_ref,
    out_ref,
    padded,
    slab,
    lookup,
    order,
    step_x,
    rim_x,
    step_y,
    spread,
    grad_x,
    grad_y,
    chosen,
    params,
    outbox,
    inbox,
    load_sem,
    halo_send,
    halo_recv,
    send_sem,
    recv_sem,
    own_sem,
):
    depth_count, height, width = volume_ref.shape
    cells = index_ref.shape[1]
    piece = height // ranks
    half = ranks // 2
    me = lax.axis_index("depth")
    tile = lax.axis_index("tile")
    col_bit = lax.rem(tile, 2)
    row_bit = lax.div(tile, 2)
    col_partner = tile + 1 - 2 * col_bit
    row_partner = lax.rem(tile + 2, tiles)
    local = lax.rem(me, half)
    side = lax.div(me, half)

    load = pltpu.make_async_copy(volume_ref, padded.at[:, pl.ds(ROWS, height), :], load_sem)
    load.start()

    barrier = pltpu.get_barrier_semaphore()

    def greet(apart, carry):
        other = lax.rem(me + apart, ranks)
        pl.semaphore_signal(barrier, inc=1, device_id=(other, tile), device_id_type=MESH)
        return carry

    lax.fori_loop(1, ranks, greet, 0)
    pl.semaphore_signal(barrier, inc=1, device_id=(me, col_partner), device_id_type=MESH)
    pl.semaphore_signal(barrier, inc=1, device_id=(me, row_partner), device_id_type=MESH)
    pl.semaphore_wait(barrier, ranks + 1)

    edge_row = pl.multiple_of((1 - row_bit) * (height - ROWS), ROWS)
    edge_col = pl.multiple_of((1 - col_bit) * (width - LANES), LANES)
    blank_row = pl.multiple_of(row_bit * (height + ROWS), ROWS)
    got_row = pl.multiple_of((1 - row_bit) * (height + ROWS), ROWS)
    send_row = pltpu.make_async_remote_copy(
        src_ref=volume_ref.at[:, pl.ds(edge_row, ROWS), :],
        dst_ref=padded.at[:, pl.ds(blank_row, ROWS), :],
        send_sem=halo_send.at[0],
        recv_sem=halo_recv.at[0],
        device_id=(me, row_partner),
        device_id_type=MESH,
    )
    send_row.start()
    send_col = pltpu.make_async_remote_copy(
        src_ref=volume_ref.at[:, :, pl.ds(edge_col, LANES)],
        dst_ref=slab,
        send_sem=halo_send.at[1],
        recv_sem=halo_recv.at[1],
        device_id=(me, col_partner),
        device_id_type=MESH,
    )
    send_col.start()
    padded[:, pl.ds(blank_row, ROWS), :] = jnp.zeros((depth_count, ROWS, width), jnp.bfloat16)

    for place in range(ranks):
        found = jnp.int32(0)
        for rank in range(ranks):
            found = jnp.where(position_ref[rank] == place, rank, found)
        order[place] = found

    def half_steps(plus, minus, shape):
        return jnp.where(plus, 0.5, jnp.where(minus, -0.5, jnp.zeros(shape, jnp.float32))).astype(jnp.bfloat16)

    from_col = lax.broadcasted_iota(jnp.int32, (width, width), 0)
    to_col = lax.broadcasted_iota(jnp.int32, (width, width), 1)
    step_x[...] = half_steps(from_col == to_col + 1, from_col == to_col - 1, (width, width))
    rim_from = lax.broadcasted_iota(jnp.int32, (LANES, width), 0)
    rim_to = lax.broadcasted_iota(jnp.int32, (LANES, width), 1)
    right_to = (1 - col_bit) * width - 1
    left_to = (col_bit - 1) * width
    rim_x[...] = half_steps(
        jnp.logical_and(rim_from == 0, rim_to == right_to),
        jnp.logical_and(rim_from == LANES - 1, rim_to == left_to),
        (LANES, width),
    )
    out_row = lax.broadcasted_iota(jnp.int32, (piece, piece + 2 * ROWS), 0) + ROWS
    in_row = lax.broadcasted_iota(jnp.int32, (piece, piece + 2 * ROWS), 1)
    step_y[...] = half_steps(in_row == out_row + 1, in_row == out_row - 1, (piece, piece + 2 * ROWS))
    cell_of = lax.rem(rim_from, cells)
    hit = jnp.logical_and(cell_of == lax.div(rim_to, CELL), rim_from < PARTS * cells)
    spread[...] = jnp.where(hit, 1.0, 0.0).astype(jnp.bfloat16)

    groups = LANES // cells

    def arrange(step, carry):
        index = index_ref[step]
        wide = jnp.concatenate([index + group * entries for group in range(groups)], axis=0)
        lookup[step] = wide.T
        return carry

    lax.fori_loop(0, depth_count, arrange, 0)

    load.wait()
    send_row.wait_send()
    send_col.wait_send()
    pltpu.make_async_remote_copy(
        src_ref=volume_ref.at[:, pl.ds(edge_row, ROWS), :],
        dst_ref=padded.at[:, pl.ds(got_row, ROWS), :],
        send_sem=halo_send.at[0],
        recv_sem=halo_recv.at[0],
        device_id=(me, row_partner),
        device_id_type=MESH,
    ).wait_recv()
    send_col.wait_recv()

    shade_x = 0.6 * math.sqrt(0.7)
    shade_y = 0.8 * math.sqrt(0.7)
    param_count = table_ref.shape[0]
    span = 2 * LANES

    def target(turn):
        far = (1 - side) * half + lax.rem(local + turn, half)
        near = side * half + lax.rem(local + turn - half + 1 + half, half)
        return jnp.where(turn < half, far, near)

    def post(turn, there):
        return pltpu.make_async_remote_copy(
            src_ref=outbox.at[turn],
            dst_ref=inbox.at[me],
            send_sem=send_sem.at[turn],
            recv_sem=recv_sem.at[me],
            device_id=(there, tile),
            device_id_type=MESH,
        )

    def block(turn, carry):
        there = target(turn)
        first = pl.multiple_of(there * piece, ROWS)

        def slopes(step, carry):
            window = padded[step, pl.ds(first, piece + 2 * ROWS), :]
            grad_y[step] = jnp.dot(step_y[...], window, preferred_element_type=jnp.float32)
            centre = padded[step, pl.ds(pl.multiple_of(first + ROWS, ROWS), piece), :]
            rim = slab[step, pl.ds(first, piece), :]
            inner = jnp.dot(centre, step_x[...], preferred_element_type=jnp.float32)
            outer = jnp.dot(rim, rim_x[...], preferred_element_type=jnp.float32)
            grad_x[step] = inner + outer
            return carry

        lax.fori_loop(0, depth_count, slopes, 0)

        def chunk(part, carry):
            row = pl.multiple_of(part * ROWS, ROWS)
            at = pl.multiple_of(first + part * ROWS, ROWS)

            def choose(step, carry):
                index = lookup[step, pl.ds(at, ROWS), :]
                for param in range(param_count):
                    table = jnp.broadcast_to(table_ref[param : param + 1, :], (ROWS, LANES))
                    value = jnp.take_along_axis(table, index, axis=1, mode="promise_in_bounds")
                    place = pl.multiple_of((step * param_count + param) * ROWS, ROWS)
                    chosen[pl.ds(place, ROWS), :] = value.astype(jnp.bfloat16)
                return carry

            lax.fori_loop(0, depth_count, choose, 0, unroll=2)
            params[...] = jnp.dot(chosen[...], spread[...], preferred_element_type=jnp.float32)

            for left in range(0, width, span):
                cols = pl.ds(left, span)

                def sample(step, carry):
                    red, green, blue, trans = carry
                    value = padded[step, pl.ds(pl.multiple_of(at + ROWS, ROWS), ROWS), cols].astype(jnp.float32)
                    gx = grad_x[step, pl.ds(row, ROWS), cols]
                    gy = grad_y[step, pl.ds(row, ROWS), cols]

                    def param(number):
                        place = pl.multiple_of((step * param_count + number) * ROWS, ROWS)
                        return params[pl.ds(place, ROWS), cols]

                    energy = gx * gx + gy * gy
                    facing = shade_x * gx + shade_y * gy
                    shade = 0.3 + facing * facing / (1.0 + energy)
                    scaled = param(0) * value - param(1)
                    keep = jnp.exp2(-(jnp.exp2(param(2) - scaled * scaled) * energy))
                    weight = trans * (1.0 - keep) * shade
                    return (
                        red + weight * param(3),
                        green + weight * param(4),
                        blue + weight * param(5),
                        trans * keep,
                    )

                zero = jnp.zeros((ROWS, span), jnp.float32)
                start = (zero, zero, zero, zero + 1.0)
                red, green, blue, trans = lax.fori_loop(0, depth_count, sample, start, unroll=3)
                for channel, image in enumerate((red, green, blue, 1.0 - trans)):
                    outbox[turn, channel, pl.ds(row, ROWS), cols] = encode(image)
            return carry

        lax.fori_loop(0, piece // ROWS, chunk, 0)

        @pl.when(turn < ranks - 1)
        def _():
            post(turn, there).start()

        return carry

    lax.fori_loop(0, ranks, block, 0)
    own = pltpu.make_async_copy(outbox.at[ranks - 1], inbox.at[me], own_sem)
    own.start()
    own.wait()

    def settle(turn, carry):
        there = target(turn)
        post(turn, there).wait_send()
        pltpu.make_async_remote_copy(
            src_ref=outbox.at[turn],
            dst_ref=inbox.at[there],
            send_sem=send_sem.at[turn],
            recv_sem=recv_sem.at[there],
            device_id=(there, tile),
            device_id_type=MESH,
        ).wait_recv()
        return carry

    lax.fori_loop(0, ranks - 1, settle, 0)

    def merge(part, carry):
        rows = pl.ds(pl.multiple_of(part * ROWS, ROWS), ROWS)
        for left in range(0, width, span):
            cols = pl.ds(left, span)

            def layer(place, images):
                rank = order[place]
                clear = 1.0 - images[3]
                return tuple(images[c] + clear * decode(inbox[rank, c, rows, cols]) for c in range(4))

            zero = jnp.zeros((ROWS, span), jnp.float32)
            images = lax.fori_loop(0, ranks, layer, (zero,) * 4, unroll=2)
            for c in range(4):
                out_ref[c, rows, cols] = images[c]
        return carry

    lax.fori_loop(0, piece // ROWS, merge, 0)


def split_tables(tables):
    parts = []
    rest = tables
    for _ in range(PARTS):
        part = lax.reduce_precision(rest, 8, 7)
        parts.append(part)
        rest = rest - part
    wide = jnp.concatenate(parts, axis=1)
    return jnp.pad(wide, ((0, 0), (0, LANES - wide.shape[1])))


def fused_device(ranks, tiles, volume, table_index, brick_position, tf_center, tf_width, tf_peak, tf_color):
    samples = volume[:, 0]
    index = jnp.swapaxes(table_index[:, 0], 1, 2)
    depth_count, height, width = samples.shape
    piece = height // ranks
    gain = math.sqrt(0.5 * LOG2E) / tf_width
    level = jnp.log2(tf_peak * (LOG2E / (depth_count * ranks)))
    tables = jnp.concatenate([gain[None], (gain * tf_center)[None], level[None], tf_color], axis=0)
    param_count = tables.shape[0]
    image = pl.pallas_call(
        functools.partial(march_kernel, ranks, tiles, tf_center.shape[0]),
        out_shape=jax.ShapeDtypeStruct((4, piece, width), jnp.float32),
        in_specs=[
            pl.BlockSpec(memory_space=pltpu.SMEM),
            pl.BlockSpec(memory_space=pltpu.VMEM),
            pl.BlockSpec(memory_space=pltpu.VMEM),
            pl.BlockSpec(memory_space=pl.ANY),
        ],
        out_specs=pl.BlockSpec(memory_space=pltpu.VMEM),
        scratch_shapes=[
            pltpu.VMEM((depth_count, height + 2 * ROWS, width), jnp.bfloat16),
            pltpu.VMEM((depth_count, height, LANES), jnp.bfloat16),
            pltpu.VMEM((depth_count, height, LANES), jnp.int32),
            pltpu.SMEM((ranks,), jnp.int32),
            pltpu.VMEM((width, width), jnp.bfloat16),
            pltpu.VMEM((LANES, width), jnp.bfloat16),
            pltpu.VMEM((piece, piece + 2 * ROWS), jnp.bfloat16),
            pltpu.VMEM((LANES, width), jnp.bfloat16),
            pltpu.VMEM((depth_count, piece, width), jnp.float32),
            pltpu.VMEM((depth_count, piece, width), jnp.float32),
            pltpu.VMEM((depth_count * param_count * ROWS, LANES), jnp.bfloat16),
            pltpu.VMEM((depth_count * param_count * ROWS, width), jnp.float32),
            pltpu.VMEM((ranks, 4, piece, width), jnp.int16),
            pltpu.VMEM((ranks, 4, piece, width), jnp.int16),
            pltpu.SemaphoreType.DMA,
            pltpu.SemaphoreType.DMA((2,)),
            pltpu.SemaphoreType.DMA((2,)),
            pltpu.SemaphoreType.DMA((ranks,)),
            pltpu.SemaphoreType.DMA((ranks,)),
            pltpu.SemaphoreType.DMA,
        ],
        compiler_params=pltpu.CompilerParams(
            collective_id=0, has_side_effects=True, vmem_limit_bytes=56 * 1024 * 1024
        ),
    )(brick_position, split_tables(tables), index, samples)
    return image[:, None]


def from_partner(value, axis, apart):
    return lax.ppermute(value, axis, [(i, i ^ 1 << apart) for i in range(lax.axis_size(axis))])


def light_sample(value, grad_x, grad_y, params, rgb, trans, inverse):
    energy = grad_x * grad_x + grad_y * grad_y
    facing = 0.6 * grad_x + 0.8 * grad_y
    shade = 0.3 + 0.7 * facing * facing / (1.0 + energy)
    scaled = (value - params[0]) / params[1]
    extinction = params[2] * jnp.exp(-0.5 * scaled * scaled) * energy * inverse
    keep = jnp.exp(-extinction)
    opacity = 1.0 - keep
    weight = trans * opacity
    rgb = rgb + weight[None] * params[3:6] * shade[None]
    trans = trans * keep
    return (rgb, trans)


def composite(layers):
    while layers.shape[1] > 1:
        front = layers[:, 0::2]
        back = layers[:, 1::2]
        layers = front + (1.0 - front[3:4]) * back
    return layers[:, 0]


def on_device(volume, table_index, brick_position, tf_center, tf_width, tf_peak, tf_color):
    tables = jnp.concatenate([tf_center[None], tf_width[None], tf_peak[None], tf_color], axis=0)
    samples = volume[:, 0]
    cells = table_index[:, 0]
    depth_count = samples.shape[0]
    height = samples.shape[1]
    width = samples.shape[2]
    cell_count = cells.shape[2]
    table_count = tables.shape[1]
    param_count = tables.shape[0]
    ranks = lax.axis_size("depth")
    inverse = 1.0 / (depth_count * ranks)
    tile_rank = lax.axis_index("tile")
    col_bit = tile_rank % 2
    row_bit = tile_rank // 2
    send_col = jnp.where(col_bit == 0, samples[:, :, width - 1], samples[:, :, 0])
    got_col = from_partner(send_col, "tile", 0)
    send_row = jnp.where(row_bit == 0, samples[:, height - 1, :], samples[:, 0, :])
    got_row = from_partner(send_row, "tile", 1)
    zero_col = jnp.zeros_like(got_col)
    zero_row = jnp.zeros_like(got_row)
    left_rim = jnp.where(col_bit == 1, got_col, zero_col)
    right_rim = jnp.where(col_bit == 0, got_col, zero_col)
    top_rim = jnp.where(row_bit == 1, got_row, zero_row)
    bottom_rim = jnp.where(row_bit == 0, got_row, zero_row)
    wide_pad = jnp.concatenate([left_rim[:, :, None], samples, right_rim[:, :, None]], axis=2)
    tall_pad = jnp.concatenate([top_rim[:, None, :], samples, bottom_rim[:, None, :]], axis=1)
    entries = jnp.arange(table_count, dtype=jnp.int32)
    table_grid = tables[:, :, None, None]

    def sample(step, carry):
        rgb, trans = carry
        wide = lax.dynamic_index_in_dim(wide_pad, step, 0, keepdims=False).astype(jnp.float32)
        tall = lax.dynamic_index_in_dim(tall_pad, step, 0, keepdims=False).astype(jnp.float32)
        cell_index = lax.dynamic_index_in_dim(cells, step, 0, keepdims=False)
        matches_cell = cell_index[None] == entries[:, None, None]
        cell_params = jnp.sum(jnp.where(matches_cell[None], table_grid, 0.0), axis=1)
        params = jnp.broadcast_to(cell_params[..., None], (param_count, height, cell_count, CELL))
        params = params.reshape(param_count, height, width)
        value = wide[:, 1:-1]
        grad_x = 0.5 * (wide[:, 2:] - wide[:, :-2])
        grad_y = 0.5 * (tall[2:, :] - tall[:-2, :])
        return light_sample(value, grad_x, grad_y, params, rgb, trans, inverse)

    start = (jnp.zeros((3, height, width), jnp.float32), jnp.ones((height, width), jnp.float32))
    rgb, trans = lax.fori_loop(0, depth_count, sample, start)
    partial_value = jnp.concatenate([rgb, (1.0 - trans)[None]], axis=0)
    piece_rows = height // ranks
    places = jnp.arange(ranks, dtype=jnp.int32)
    matches = brick_position[None, :] == places[:, None]
    rank_at = jnp.sum(jnp.where(matches, places[None, :], 0), axis=1)
    received = lax.all_to_all(partial_value, "depth", split_axis=1, concat_axis=0, tiled=True)
    stacked = received.reshape(ranks, 4, piece_rows, received.shape[2])
    ordered = jnp.take(stacked, rank_at, axis=0)
    image = composite(jnp.moveaxis(ordered, 0, 1))
    return image[:, None]


def fits(ranks, tiles, shape):
    height, width = shape[2], shape[3]
    even = ranks % 2 == 0 and tiles == 4 and height % ranks == 0
    return even and (height // ranks) % ROWS == 0 and width % (2 * LANES) == 0 and height % LANES == 0


def solution(mesh):
    ranks = mesh.shape["depth"]
    tiles = mesh.shape["tile"]

    def program(volume, *rest):
        chosen = on_device
        if fits(ranks, tiles, volume.shape):
            chosen = functools.partial(fused_device, ranks, tiles)
        return jax.shard_map(
            chosen,
            mesh=mesh,
            in_specs=(P("depth", "tile", None, None), P("depth", "tile", None, None), P(), P(), P(), P(), P()),
            out_specs=P(None, "tile", "depth", None),
            check_vma=False,
        )(volume, *rest)

    return program
```

```python
import functools
import math
import jax
import jax.numpy as jnp
from jax import lax
from jax.experimental import pallas as pl
from jax.experimental.pallas import tpu as pltpu
from jax.sharding import PartitionSpec as P

CELL = 16
ROWS = 16
LANES = 128
OCTAVES = 30.0
TOP_CODE = 65535.0
MID_CODE = 32768
SCALE = TOP_CODE / OCTAVES
LOG2E = 1.0 / math.log(2.0)
MESH = pl.DeviceIdType.MESH


def encode(value):
    code = jnp.log(value) * (-SCALE * LOG2E)
    code = jnp.minimum(jnp.maximum(code, 0.0), TOP_CODE)
    return ((code + 0.5).astype(jnp.int32) - MID_CODE).astype(jnp.int16)


def decode(code):
    steps = code.astype(jnp.int32).astype(jnp.float32)
    value = jnp.exp2((steps + float(MID_CODE)) * (-1.0 / SCALE))
    return jnp.where(steps >= TOP_CODE - MID_CODE, 0.0, value)


def march_kernel(
    ranks,
    tiles,
    position_ref,
    center_ref,
    width_ref,
    peak_ref,
    color_ref,
    index_ref,
    volume_ref,
    out_ref,
    padded,
    slab,
    lookup,
    order,
    step_x,
    rim_x,
    step_y,
    tables,
    grad_x,
    grad_y,
    outbox,
    inbox,
    load_sem,
    halo_send,
    halo_recv,
    send_sem,
    recv_sem,
    own_sem,
):
    depth_count, height, width = volume_ref.shape
    cells = index_ref.shape[1]
    piece = height // ranks
    half = ranks // 2
    me = lax.axis_index("depth")
    tile = lax.axis_index("tile")
    col_bit = lax.rem(tile, 2)
    row_bit = lax.div(tile, 2)
    col_partner = tile + 1 - 2 * col_bit
    row_partner = lax.rem(tile + 2, tiles)
    local = lax.rem(me, half)
    side = lax.div(me, half)

    load = pltpu.make_async_copy(volume_ref, padded.at[:, pl.ds(ROWS, height), :], load_sem)
    load.start()

    barrier = pltpu.get_barrier_semaphore()

    def greet(apart, carry):
        other = lax.rem(me + apart, ranks)
        pl.semaphore_signal(barrier, inc=1, device_id=(other, tile), device_id_type=MESH)
        return carry

    lax.fori_loop(1, ranks, greet, 0)
    pl.semaphore_signal(barrier, inc=1, device_id=(me, col_partner), device_id_type=MESH)
    pl.semaphore_signal(barrier, inc=1, device_id=(me, row_partner), device_id_type=MESH)
    pl.semaphore_wait(barrier, ranks + 1)

    edge_row = pl.multiple_of((1 - row_bit) * (height - ROWS), ROWS)
    edge_col = pl.multiple_of((1 - col_bit) * (width - LANES), LANES)
    blank_row = pl.multiple_of(row_bit * (height + ROWS), ROWS)
    got_row = pl.multiple_of((1 - row_bit) * (height + ROWS), ROWS)
    send_row = pltpu.make_async_remote_copy(
        src_ref=volume_ref.at[:, pl.ds(edge_row, ROWS), :],
        dst_ref=padded.at[:, pl.ds(blank_row, ROWS), :],
        send_sem=halo_send.at[0],
        recv_sem=halo_recv.at[0],
        device_id=(me, row_partner),
        device_id_type=MESH,
    )
    send_row.start()
    send_col = pltpu.make_async_remote_copy(
        src_ref=volume_ref.at[:, :, pl.ds(edge_col, LANES)],
        dst_ref=slab,
        send_sem=halo_send.at[1],
        recv_sem=halo_recv.at[1],
        device_id=(me, col_partner),
        device_id_type=MESH,
    )
    send_col.start()
    padded[:, pl.ds(blank_row, ROWS), :] = jnp.zeros((depth_count, ROWS, width), jnp.bfloat16)

    for place in range(ranks):
        found = jnp.int32(0)
        for rank in range(ranks):
            found = jnp.where(position_ref[rank] == place, rank, found)
        order[place] = found

    def half_steps(plus, minus, shape):
        return jnp.where(plus, 0.5, jnp.where(minus, -0.5, jnp.zeros(shape, jnp.float32))).astype(jnp.bfloat16)

    from_col = lax.broadcasted_iota(jnp.int32, (width, width), 0)
    to_col = lax.broadcasted_iota(jnp.int32, (width, width), 1)
    step_x[...] = half_steps(from_col == to_col + 1, from_col == to_col - 1, (width, width))
    rim_from = lax.broadcasted_iota(jnp.int32, (LANES, width), 0)
    rim_to = lax.broadcasted_iota(jnp.int32, (LANES, width), 1)
    right_to = (1 - col_bit) * width - 1
    left_to = (col_bit - 1) * width
    rim_x[...] = half_steps(
        jnp.logical_and(rim_from == 0, rim_to == right_to),
        jnp.logical_and(rim_from == LANES - 1, rim_to == left_to),
        (LANES, width),
    )
    out_row = lax.broadcasted_iota(jnp.int32, (piece, piece + 2 * ROWS), 0) + ROWS
    in_row = lax.broadcasted_iota(jnp.int32, (piece, piece + 2 * ROWS), 1)
    step_y[...] = half_steps(in_row == out_row + 1, in_row == out_row - 1, (piece, piece + 2 * ROWS))
    entries = center_ref.shape[1]
    gain = math.sqrt(0.5 * LOG2E) / width_ref[...]
    level = jnp.log(peak_ref[...] * (LOG2E / (depth_count * ranks))) * LOG2E
    tables[...] = jnp.zeros(tables.shape, jnp.float32)
    tables[0:1, 0:entries] = gain
    tables[1:2, 0:entries] = gain * center_ref[...]
    tables[2:3, 0:entries] = level
    tables[3:6, 0:entries] = color_ref[...]

    groups = LANES // cells

    def arrange(step, carry):
        index = index_ref[step]
        wide = jnp.concatenate([index] * groups, axis=0)
        lookup[step] = wide.T
        return carry

    lax.fori_loop(0, depth_count, arrange, 0)

    load.wait()
    send_row.wait_send()
    send_col.wait_send()
    pltpu.make_async_remote_copy(
        src_ref=volume_ref.at[:, pl.ds(edge_row, ROWS), :],
        dst_ref=padded.at[:, pl.ds(got_row, ROWS), :],
        send_sem=halo_send.at[0],
        recv_sem=halo_recv.at[0],
        device_id=(me, row_partner),
        device_id_type=MESH,
    ).wait_recv()
    send_col.wait_recv()

    shade_x = 0.6 * math.sqrt(0.7)
    shade_y = 0.8 * math.sqrt(0.7)
    cell_pattern = lax.div(lax.broadcasted_iota(jnp.int32, (ROWS, LANES), 1), CELL)
    cells_across = LANES // CELL

    def target(turn):
        far = (1 - side) * half + lax.rem(local + turn, half)
        near = side * half + lax.rem(local + turn - half + 1 + half, half)
        return jnp.where(turn < half, far, near)

    def post(turn, there):
        return pltpu.make_async_remote_copy(
            src_ref=outbox.at[turn],
            dst_ref=inbox.at[me],
            send_sem=send_sem.at[turn],
            recv_sem=recv_sem.at[me],
            device_id=(there, tile),
            device_id_type=MESH,
        )

    def block(turn, carry):
        there = target(turn)
        first = pl.multiple_of(there * piece, ROWS)

        def slopes(step, carry):
            window = padded[step, pl.ds(first, piece + 2 * ROWS), :]
            grad_y[step] = jnp.dot(step_y[...], window, preferred_element_type=jnp.float32)
            return carry

        lax.fori_loop(0, depth_count, slopes, 0, unroll=2)
        centre = padded[:, pl.ds(pl.multiple_of(first + ROWS, ROWS), piece), :].reshape(depth_count * piece, width)
        rim = slab[:, pl.ds(first, piece), :].reshape(depth_count * piece, LANES)
        inner = jnp.dot(centre, step_x[...], preferred_element_type=jnp.float32)
        outer = jnp.dot(rim, rim_x[...], preferred_element_type=jnp.float32)
        grad_x[...] = (inner + outer).reshape(depth_count, piece, width)

        def chunk(part, carry):
            row = pl.multiple_of(part * ROWS, ROWS)
            at = pl.multiple_of(first + part * ROWS, ROWS)
            rows = [jnp.broadcast_to(tables[p : p + 1, :], (ROWS, LANES)) for p in range(6)]

            for left in range(0, width, LANES):
                cols = pl.ds(left, LANES)
                pattern = cell_pattern + left // LANES * cells_across

                def sample(step, carry):
                    red, green, blue, trans = carry
                    value = padded[step, pl.ds(pl.multiple_of(at + ROWS, ROWS), ROWS), cols].astype(jnp.float32)
                    gx = grad_x[step, pl.ds(row, ROWS), cols]
                    gy = grad_y[step, pl.ds(row, ROWS), cols]
                    cell = lookup[step, pl.ds(at, ROWS), :]
                    index = jnp.take_along_axis(cell, pattern, axis=1, mode="promise_in_bounds")

                    def param(number):
                        return jnp.take_along_axis(rows[number], index, axis=1, mode="promise_in_bounds")

                    energy = gx * gx + gy * gy
                    facing = shade_x * gx + shade_y * gy
                    base = 1.0 + energy
                    rough = pl.reciprocal(base, approx=True)
                    shade = 0.3 + facing * facing * (rough * (2.0 - base * rough))
                    scaled = param(0) * value - param(1)
                    keep = jnp.exp2(-(jnp.exp2(param(2) - scaled * scaled) * energy))
                    weight = trans * (1.0 - keep) * shade
                    return (
                        red + weight * param(3),
                        green + weight * param(4),
                        blue + weight * param(5),
                        trans * keep,
                    )

                zero = jnp.zeros((ROWS, LANES), jnp.float32)
                start = (zero, zero, zero, zero + 1.0)
                red, green, blue, trans = lax.fori_loop(0, depth_count, sample, start, unroll=6)
                for channel, image in enumerate((red, green, blue, 1.0 - trans)):
                    outbox[turn, channel, pl.ds(row, ROWS), cols] = encode(image)
            return carry

        lax.fori_loop(0, piece // ROWS, chunk, 0)

        @pl.when(turn < ranks - 1)
        def _():
            post(turn, there).start()

        return carry

    lax.fori_loop(0, ranks, block, 0)
    own = pltpu.make_async_copy(outbox.at[ranks - 1], inbox.at[me], own_sem)
    own.start()
    own.wait()

    def settle(turn, carry):
        there = target(turn)
        post(turn, there).wait_send()
        pltpu.make_async_remote_copy(
            src_ref=outbox.at[turn],
            dst_ref=inbox.at[there],
            send_sem=send_sem.at[turn],
            recv_sem=recv_sem.at[there],
            device_id=(there, tile),
            device_id_type=MESH,
        ).wait_recv()
        return carry

    lax.fori_loop(0, ranks - 1, settle, 0)

    span = 2 * LANES

    def merge(part, carry):
        rows = pl.ds(pl.multiple_of(part * ROWS, ROWS), ROWS)
        for left in range(0, width, span):
            cols = pl.ds(left, span)

            def layer(place, images):
                rank = order[place]
                clear = 1.0 - images[3]
                return tuple(images[c] + clear * decode(inbox[rank, c, rows, cols]) for c in range(4))

            zero = jnp.zeros((ROWS, span), jnp.float32)
            images = lax.fori_loop(0, ranks, layer, (zero,) * 4, unroll=2)
            for c in range(4):
                out_ref[c, rows, cols] = images[c]
        return carry

    lax.fori_loop(0, piece // ROWS, merge, 0)


def fused_device(ranks, tiles, volume, table_index, brick_position, tf_center, tf_width, tf_peak, tf_color):
    samples = volume[:, 0]
    index = jnp.swapaxes(table_index[:, 0], 1, 2)
    depth_count, height, width = samples.shape
    piece = height // ranks
    image = pl.pallas_call(
        functools.partial(march_kernel, ranks, tiles),
        out_shape=jax.ShapeDtypeStruct((4, piece, width), jnp.float32),
        in_specs=[
            pl.BlockSpec(memory_space=pltpu.SMEM),
            pl.BlockSpec(memory_space=pltpu.VMEM),
            pl.BlockSpec(memory_space=pltpu.VMEM),
            pl.BlockSpec(memory_space=pltpu.VMEM),
            pl.BlockSpec(memory_space=pltpu.VMEM),
            pl.BlockSpec(memory_space=pltpu.VMEM),
            pl.BlockSpec(memory_space=pl.ANY),
        ],
        out_specs=pl.BlockSpec(memory_space=pltpu.VMEM),
        scratch_shapes=[
            pltpu.VMEM((depth_count, height + 2 * ROWS, width), jnp.bfloat16),
            pltpu.VMEM((depth_count, height, LANES), jnp.bfloat16),
            pltpu.VMEM((depth_count, height, LANES), jnp.int32),
            pltpu.SMEM((ranks,), jnp.int32),
            pltpu.VMEM((width, width), jnp.bfloat16),
            pltpu.VMEM((LANES, width), jnp.bfloat16),
            pltpu.VMEM((piece, piece + 2 * ROWS), jnp.bfloat16),
            pltpu.VMEM((8, LANES), jnp.float32),
            pltpu.VMEM((depth_count, piece, width), jnp.float32),
            pltpu.VMEM((depth_count, piece, width), jnp.float32),
            pltpu.VMEM((ranks, 4, piece, width), jnp.int16),
            pltpu.VMEM((ranks, 4, piece, width), jnp.int16),
            pltpu.SemaphoreType.DMA,
            pltpu.SemaphoreType.DMA((2,)),
            pltpu.SemaphoreType.DMA((2,)),
            pltpu.SemaphoreType.DMA((ranks,)),
            pltpu.SemaphoreType.DMA((ranks,)),
            pltpu.SemaphoreType.DMA,
        ],
        compiler_params=pltpu.CompilerParams(
            collective_id=0, has_side_effects=True, vmem_limit_bytes=56 * 1024 * 1024
        ),
    )(brick_position, tf_center[None], tf_width[None], tf_peak[None], tf_color, index, samples)
    return image[:, None]


def from_partner(value, axis, apart):
    return lax.ppermute(value, axis, [(i, i ^ 1 << apart) for i in range(lax.axis_size(axis))])


def light_sample(value, grad_x, grad_y, params, rgb, trans, inverse):
    energy = grad_x * grad_x + grad_y * grad_y
    facing = 0.6 * grad_x + 0.8 * grad_y
    shade = 0.3 + 0.7 * facing * facing / (1.0 + energy)
    scaled = (value - params[0]) / params[1]
    extinction = params[2] * jnp.exp(-0.5 * scaled * scaled) * energy * inverse
    keep = jnp.exp(-extinction)
    opacity = 1.0 - keep
    weight = trans * opacity
    rgb = rgb + weight[None] * params[3:6] * shade[None]
    trans = trans * keep
    return (rgb, trans)


def composite(layers):
    while layers.shape[1] > 1:
        front = layers[:, 0::2]
        back = layers[:, 1::2]
        layers = front + (1.0 - front[3:4]) * back
    return layers[:, 0]


def on_device(volume, table_index, brick_position, tf_center, tf_width, tf_peak, tf_color):
    tables = jnp.concatenate([tf_center[None], tf_width[None], tf_peak[None], tf_color], axis=0)
    samples = volume[:, 0]
    cells = table_index[:, 0]
    depth_count = samples.shape[0]
    height = samples.shape[1]
    width = samples.shape[2]
    cell_count = cells.shape[2]
    table_count = tables.shape[1]
    param_count = tables.shape[0]
    ranks = lax.axis_size("depth")
    inverse = 1.0 / (depth_count * ranks)
    tile_rank = lax.axis_index("tile")
    col_bit = tile_rank % 2
    row_bit = tile_rank // 2
    send_col = jnp.where(col_bit == 0, samples[:, :, width - 1], samples[:, :, 0])
    got_col = from_partner(send_col, "tile", 0)
    send_row = jnp.where(row_bit == 0, samples[:, height - 1, :], samples[:, 0, :])
    got_row = from_partner(send_row, "tile", 1)
    zero_col = jnp.zeros_like(got_col)
    zero_row = jnp.zeros_like(got_row)
    left_rim = jnp.where(col_bit == 1, got_col, zero_col)
    right_rim = jnp.where(col_bit == 0, got_col, zero_col)
    top_rim = jnp.where(row_bit == 1, got_row, zero_row)
    bottom_rim = jnp.where(row_bit == 0, got_row, zero_row)
    wide_pad = jnp.concatenate([left_rim[:, :, None], samples, right_rim[:, :, None]], axis=2)
    tall_pad = jnp.concatenate([top_rim[:, None, :], samples, bottom_rim[:, None, :]], axis=1)
    entries = jnp.arange(table_count, dtype=jnp.int32)
    table_grid = tables[:, :, None, None]

    def sample(step, carry):
        rgb, trans = carry
        wide = lax.dynamic_index_in_dim(wide_pad, step, 0, keepdims=False).astype(jnp.float32)
        tall = lax.dynamic_index_in_dim(tall_pad, step, 0, keepdims=False).astype(jnp.float32)
        cell_index = lax.dynamic_index_in_dim(cells, step, 0, keepdims=False)
        matches_cell = cell_index[None] == entries[:, None, None]
        cell_params = jnp.sum(jnp.where(matches_cell[None], table_grid, 0.0), axis=1)
        params = jnp.broadcast_to(cell_params[..., None], (param_count, height, cell_count, CELL))
        params = params.reshape(param_count, height, width)
        value = wide[:, 1:-1]
        grad_x = 0.5 * (wide[:, 2:] - wide[:, :-2])
        grad_y = 0.5 * (tall[2:, :] - tall[:-2, :])
        return light_sample(value, grad_x, grad_y, params, rgb, trans, inverse)

    start = (jnp.zeros((3, height, width), jnp.float32), jnp.ones((height, width), jnp.float32))
    rgb, trans = lax.fori_loop(0, depth_count, sample, start)
    partial_value = jnp.concatenate([rgb, (1.0 - trans)[None]], axis=0)
    piece_rows = height // ranks
    places = jnp.arange(ranks, dtype=jnp.int32)
    matches = brick_position[None, :] == places[:, None]
    rank_at = jnp.sum(jnp.where(matches, places[None, :], 0), axis=1)
    received = lax.all_to_all(partial_value, "depth", split_axis=1, concat_axis=0, tiled=True)
    stacked = received.reshape(ranks, 4, piece_rows, received.shape[2])
    ordered = jnp.take(stacked, rank_at, axis=0)
    image = composite(jnp.moveaxis(ordered, 0, 1))
    return image[:, None]


def fits(ranks, tiles, shape):
    height, width = shape[2], shape[3]
    even = ranks % 2 == 0 and tiles == 4 and height % ranks == 0
    return even and (height // ranks) % ROWS == 0 and width % (2 * LANES) == 0 and height % LANES == 0


def solution(mesh):
    ranks = mesh.shape["depth"]
    tiles = mesh.shape["tile"]

    def program(volume, *rest):
        chosen = on_device
        if fits(ranks, tiles, volume.shape):
            chosen = functools.partial(fused_device, ranks, tiles)
        return jax.shard_map(
            chosen,
            mesh=mesh,
            in_specs=(P("depth", "tile", None, None), P("depth", "tile", None, None), P(), P(), P(), P(), P()),
            out_specs=P(None, "tile", "depth", None),
            check_vma=False,
        )(volume, *rest)

    return program
```

```python
import functools
import math
import jax
import jax.numpy as jnp
from jax import lax
from jax.experimental import pallas as pl
from jax.experimental.pallas import tpu as pltpu
from jax.sharding import PartitionSpec as P

CELL = 16
ROWS = 16
LANES = 128
RIM = 8
OCTAVES = 30.0
TOP_CODE = 65535.0
MID_CODE = 32768
SCALE = TOP_CODE / OCTAVES
LOG2E = 1.0 / math.log(2.0)
MESH = pl.DeviceIdType.MESH


def encode(value):
    code = jnp.log(value) * (-SCALE * LOG2E)
    code = jnp.minimum(jnp.maximum(code, 0.0), TOP_CODE)
    return ((code + 0.5).astype(jnp.int32) - MID_CODE).astype(jnp.int16)


def decode(code):
    steps = code.astype(jnp.int32).astype(jnp.float32)
    value = jnp.exp2((steps + float(MID_CODE)) * (-1.0 / SCALE))
    return jnp.where(steps >= TOP_CODE - MID_CODE, 0.0, value)


def march_kernel(
    ranks,
    tiles,
    position_ref,
    center_ref,
    width_ref,
    peak_ref,
    color_ref,
    index_ref,
    volume_ref,
    out_ref,
    padded,
    slab,
    order,
    half_eye,
    rim_pick,
    step_y,
    tables,
    turned,
    grad_y,
    cell_params,
    image_turned,
    outbox,
    inbox,
    load_sem,
    halo_send,
    halo_recv,
    send_sem,
    recv_sem,
    own_sem,
):
    depth_count, height, width = volume_ref.shape
    cells = index_ref.shape[1]
    span = half_eye.shape[0]
    window = step_y.shape[0]
    piece = height // ranks
    half = ranks // 2
    me = lax.axis_index("depth")
    tile = lax.axis_index("tile")
    col_bit = lax.rem(tile, 2)
    row_bit = lax.div(tile, 2)
    col_partner = tile + 1 - 2 * col_bit
    row_partner = lax.rem(tile + 2, tiles)
    side = lax.div(me, half)

    load = pltpu.make_async_copy(volume_ref, padded.at[:, pl.ds(ROWS, height), :], load_sem)
    load.start()

    barrier = pltpu.get_barrier_semaphore()

    def greet(apart, carry):
        other = lax.rem(me + apart, ranks)
        pl.semaphore_signal(barrier, inc=1, device_id=(other, tile), device_id_type=MESH)
        return carry

    lax.fori_loop(1, ranks, greet, 0)
    pl.semaphore_signal(barrier, inc=1, device_id=(me, col_partner), device_id_type=MESH)
    pl.semaphore_signal(barrier, inc=1, device_id=(me, row_partner), device_id_type=MESH)
    pl.semaphore_wait(barrier, ranks + 1)

    edge_row = pl.multiple_of((1 - row_bit) * (height - ROWS), ROWS)
    edge_col = pl.multiple_of((1 - col_bit) * (width - LANES), LANES)
    blank_row = pl.multiple_of(row_bit * (height + ROWS), ROWS)
    got_row = pl.multiple_of((1 - row_bit) * (height + ROWS), ROWS)
    send_row = pltpu.make_async_remote_copy(
        src_ref=volume_ref.at[:, pl.ds(edge_row, ROWS), :],
        dst_ref=padded.at[:, pl.ds(blank_row, ROWS), :],
        send_sem=halo_send.at[0],
        recv_sem=halo_recv.at[0],
        device_id=(me, row_partner),
        device_id_type=MESH,
    )
    send_row.start()
    send_col = pltpu.make_async_remote_copy(
        src_ref=volume_ref.at[:, :, pl.ds(edge_col, LANES)],
        dst_ref=slab,
        send_sem=halo_send.at[1],
        recv_sem=halo_recv.at[1],
        device_id=(me, col_partner),
        device_id_type=MESH,
    )
    send_col.start()
    padded[:, pl.ds(blank_row, ROWS), :] = jnp.zeros((depth_count, ROWS, width), jnp.bfloat16)

    for place in range(ranks):
        found = jnp.int32(0)
        for rank in range(ranks):
            found = jnp.where(position_ref[rank] == place, rank, found)
        order[place] = found

    def from_mask(mask, number):
        return jnp.where(mask, number, 0.0).astype(jnp.bfloat16)

    eye_row = lax.broadcasted_iota(jnp.int32, (span, span), 0)
    eye_col = lax.broadcasted_iota(jnp.int32, (span, span), 1)
    half_eye[...] = from_mask(eye_row == eye_col, 0.5)
    pick_row = lax.broadcasted_iota(jnp.int32, (ROWS, LANES), 0)
    pick_col = lax.broadcasted_iota(jnp.int32, (ROWS, LANES), 1)
    wanted_row = jnp.where(col_bit == 1, RIM - 1, RIM)
    wanted_col = jnp.where(col_bit == 1, LANES - 1, 0)
    rim_pick[...] = from_mask(jnp.logical_and(pick_row == wanted_row, pick_col == wanted_col), 0.5)
    window_row = lax.broadcasted_iota(jnp.int32, (window, LANES), 0)
    window_at = jnp.where(window_row < LANES, window_row, jnp.where(window_row < LANES + ROWS, window_row - LANES - ROWS, window_row - ROWS))
    lane_at = lax.broadcasted_iota(jnp.int32, (window, LANES), 1)
    plus = from_mask(window_at == lane_at + 1, 1.0)
    step_y[...] = plus - from_mask(window_at == lane_at - 1, 1.0)

    entries = center_ref.shape[1]
    gain = math.sqrt(0.5 * LOG2E) / width_ref[...]
    level = jnp.log(peak_ref[...] * (LOG2E / (depth_count * ranks))) * LOG2E
    tables[...] = jnp.zeros(tables.shape, jnp.float32)
    tables[0:1, 0:entries] = gain + gain
    tables[1:2, 0:entries] = gain * center_ref[...]
    tables[2:3, 0:entries] = level
    tables[3:6, 0:entries] = color_ref[...]

    load.wait()
    send_row.wait_send()
    send_col.wait_send()
    pltpu.make_async_remote_copy(
        src_ref=volume_ref.at[:, pl.ds(edge_row, ROWS), :],
        dst_ref=padded.at[:, pl.ds(got_row, ROWS), :],
        send_sem=halo_send.at[0],
        recv_sem=halo_recv.at[0],
        device_id=(me, row_partner),
        device_id_type=MESH,
    ).wait_recv()
    send_col.wait_recv()

    shade_x = 0.6 * math.sqrt(0.7)
    shade_y = 0.8 * math.sqrt(0.7)
    def post(there):
        return pltpu.make_async_remote_copy(
            src_ref=outbox.at[:, pl.ds(pl.multiple_of(there * piece, ROWS), piece), :],
            dst_ref=inbox.at[me],
            send_sem=send_sem.at[there],
            recv_sem=recv_sem.at[me],
            device_id=(there, tile),
            device_id_type=MESH,
        )

    blocks = height // LANES // 2
    transposed = (((1,), (1,)), ((), ()))

    def block(turn, carry):
        away = 1 - lax.div(turn, blocks)
        part = lax.rem(turn, blocks)
        area = lax.rem(side + away, 2)
        first = pl.multiple_of((area * blocks + part) * LANES, LANES)
        entry_rows = [jnp.broadcast_to(tables[p : p + 1, :], (cells, LANES)) for p in range(6)]

        def prepare(step, carry):
            index = index_ref[step, :, pl.ds(first, LANES)]
            for p in range(6):
                found = jnp.take_along_axis(entry_rows[p], index, axis=1, mode="promise_in_bounds")
                cell_params[step, p * cells : (p + 1) * cells, :] = found
            for left in range(0, width, span):
                cols = pl.ds(left, span)
                near = padded[step, pl.ds(pl.multiple_of(first + ROWS, ROWS), LANES), cols]
                above = padded[step, pl.ds(first, ROWS), cols]
                below = padded[step, pl.ds(pl.multiple_of(first + ROWS + LANES, ROWS), ROWS), cols]
                rows = jnp.concatenate([near, above, below], axis=0)
                flipped = lax.dot_general(half_eye[...], rows, transposed, preferred_element_type=jnp.float32)
                turned[step, RIM + left : RIM + left + span, :] = flipped[:, :LANES]
                grad_y[step, cols, :] = jnp.dot(
                    flipped.astype(jnp.bfloat16), step_y[...], preferred_element_type=jnp.float32
                )
            rim = slab[step, pl.ds(first, LANES), :]
            edges = lax.dot_general(rim_pick[...], rim, transposed, preferred_element_type=jnp.float32)
            turned[step, 0:RIM, :] = edges[:RIM]
            turned[step, RIM + width : 2 * RIM + width, :] = edges[RIM:]
            return carry

        lax.fori_loop(0, depth_count, prepare, 0, unroll=2)

        def column(cell, carry):
            top = pl.multiple_of(cell * CELL, CELL)

            def sample(step, carry):
                red, green, blue, trans = carry
                value = turned[step, pl.ds(top + RIM, CELL), :]
                gx = turned[step, pl.ds(top + RIM + 1, CELL), :] - turned[step, pl.ds(top + RIM - 1, CELL), :]
                gy = grad_y[step, pl.ds(top, CELL), :]

                def param(number):
                    row = cell_params[step, pl.ds(number * cells + cell, 1), :]
                    return jnp.broadcast_to(row, (CELL, LANES))

                energy = gx * gx + gy * gy
                facing = shade_x * gx + shade_y * gy
                base = 1.0 + energy
                rough = pl.reciprocal(base, approx=True)
                shade = 0.3 + facing * facing * (rough * (2.0 - base * rough))
                scaled = param(0) * value - param(1)
                keep = jnp.exp2(-(jnp.exp2(param(2) - scaled * scaled) * energy))
                weight = trans * (1.0 - keep) * shade
                return (
                    red + weight * param(3),
                    green + weight * param(4),
                    blue + weight * param(5),
                    trans * keep,
                )

            zero = jnp.zeros((CELL, LANES), jnp.float32)
            start = (zero, zero, zero, zero + 1.0)
            red, green, blue, trans = lax.fori_loop(0, depth_count, sample, start, unroll=True)
            for channel, image in enumerate((red, green, blue, 1.0 - trans)):
                image_turned[channel, pl.ds(top, CELL), :] = image
            return carry

        lax.fori_loop(0, cells, column, 0)

        for channel in range(4):
            for left in range(0, width, LANES):
                flat = image_turned[channel, left : left + LANES, :].T
                outbox[channel, pl.ds(first, LANES), left : left + LANES] = encode(flat)

        def dispatch(number, carry):
            there = area * half + number

            @pl.when(there != me)
            def _():
                post(there).start()

            return carry

        lax.fori_loop(part * LANES // piece, (part + 1) * LANES // piece, dispatch, 0)
        return carry

    lax.fori_loop(0, 2 * blocks, block, 0)
    mine = outbox.at[:, pl.ds(pl.multiple_of(me * piece, ROWS), piece), :]
    own = pltpu.make_async_copy(mine, inbox.at[me], own_sem)
    own.start()
    own.wait()

    def settle(apart, carry):
        there = lax.rem(me + apart, ranks)
        post(there).wait_send()
        pltpu.make_async_remote_copy(
            src_ref=mine,
            dst_ref=inbox.at[there],
            send_sem=send_sem.at[there],
            recv_sem=recv_sem.at[there],
            device_id=(there, tile),
            device_id_type=MESH,
        ).wait_recv()
        return carry

    lax.fori_loop(1, ranks, settle, 0)

    def merge(part, carry):
        rows = pl.ds(pl.multiple_of(part * ROWS, ROWS), ROWS)
        for left in range(0, width, span):
            cols = pl.ds(left, span)

            def layer(place, images):
                rank = order[place]
                clear = 1.0 - images[3]
                return tuple(images[c] + clear * decode(inbox[rank, c, rows, cols]) for c in range(4))

            zero = jnp.zeros((ROWS, span), jnp.float32)
            images = lax.fori_loop(0, ranks, layer, (zero,) * 4, unroll=2)
            for c in range(4):
                out_ref[c, rows, cols] = images[c]
        return carry

    lax.fori_loop(0, piece // ROWS, merge, 0)


def fused_device(ranks, tiles, volume, table_index, brick_position, tf_center, tf_width, tf_peak, tf_color):
    samples = volume[:, 0]
    index = jnp.swapaxes(table_index[:, 0], 1, 2)
    depth_count, height, width = samples.shape
    piece = height // ranks
    cells = index.shape[1]
    image = pl.pallas_call(
        functools.partial(march_kernel, ranks, tiles),
        out_shape=jax.ShapeDtypeStruct((4, piece, width), jnp.float32),
        in_specs=[
            pl.BlockSpec(memory_space=pltpu.SMEM),
            pl.BlockSpec(memory_space=pltpu.VMEM),
            pl.BlockSpec(memory_space=pltpu.VMEM),
            pl.BlockSpec(memory_space=pltpu.VMEM),
            pl.BlockSpec(memory_space=pltpu.VMEM),
            pl.BlockSpec(memory_space=pltpu.VMEM),
            pl.BlockSpec(memory_space=pl.ANY),
        ],
        out_specs=pl.BlockSpec(memory_space=pltpu.VMEM),
        scratch_shapes=[
            pltpu.VMEM((depth_count, height + 2 * ROWS, width), jnp.bfloat16),
            pltpu.VMEM((depth_count, height, LANES), jnp.bfloat16),
            pltpu.SMEM((ranks,), jnp.int32),
            pltpu.VMEM((2 * LANES, 2 * LANES), jnp.bfloat16),
            pltpu.VMEM((ROWS, LANES), jnp.bfloat16),
            pltpu.VMEM((LANES + 2 * ROWS, LANES), jnp.bfloat16),
            pltpu.VMEM((8, LANES), jnp.float32),
            pltpu.VMEM((depth_count, width + 2 * RIM, LANES), jnp.float32),
            pltpu.VMEM((depth_count, width, LANES), jnp.float32),
            pltpu.VMEM((depth_count, 6 * cells, LANES), jnp.float32),
            pltpu.VMEM((4, width, LANES), jnp.float32),
            pltpu.VMEM((4, height, width), jnp.int16),
            pltpu.VMEM((ranks, 4, piece, width), jnp.int16),
            pltpu.SemaphoreType.DMA,
            pltpu.SemaphoreType.DMA((2,)),
            pltpu.SemaphoreType.DMA((2,)),
            pltpu.SemaphoreType.DMA((ranks,)),
            pltpu.SemaphoreType.DMA((ranks,)),
            pltpu.SemaphoreType.DMA,
        ],
        compiler_params=pltpu.CompilerParams(
            collective_id=0, has_side_effects=True, vmem_limit_bytes=56 * 1024 * 1024
        ),
    )(brick_position, tf_center[None], tf_width[None], tf_peak[None], tf_color, index, samples)
    return image[:, None]


def from_partner(value, axis, apart):
    return lax.ppermute(value, axis, [(i, i ^ 1 << apart) for i in range(lax.axis_size(axis))])


def light_sample(value, grad_x, grad_y, params, rgb, trans, inverse):
    energy = grad_x * grad_x + grad_y * grad_y
    facing = 0.6 * grad_x + 0.8 * grad_y
    shade = 0.3 + 0.7 * facing * facing / (1.0 + energy)
    scaled = (value - params[0]) / params[1]
    extinction = params[2] * jnp.exp(-0.5 * scaled * scaled) * energy * inverse
    keep = jnp.exp(-extinction)
    opacity = 1.0 - keep
    weight = trans * opacity
    rgb = rgb + weight[None] * params[3:6] * shade[None]
    trans = trans * keep
    return (rgb, trans)


def composite(layers):
    while layers.shape[1] > 1:
        front = layers[:, 0::2]
        back = layers[:, 1::2]
        layers = front + (1.0 - front[3:4]) * back
    return layers[:, 0]


def on_device(volume, table_index, brick_position, tf_center, tf_width, tf_peak, tf_color):
    tables = jnp.concatenate([tf_center[None], tf_width[None], tf_peak[None], tf_color], axis=0)
    samples = volume[:, 0]
    cells = table_index[:, 0]
    depth_count = samples.shape[0]
    height = samples.shape[1]
    width = samples.shape[2]
    cell_count = cells.shape[2]
    table_count = tables.shape[1]
    param_count = tables.shape[0]
    ranks = lax.axis_size("depth")
    inverse = 1.0 / (depth_count * ranks)
    tile_rank = lax.axis_index("tile")
    col_bit = tile_rank % 2
    row_bit = tile_rank // 2
    send_col = jnp.where(col_bit == 0, samples[:, :, width - 1], samples[:, :, 0])
    got_col = from_partner(send_col, "tile", 0)
    send_row = jnp.where(row_bit == 0, samples[:, height - 1, :], samples[:, 0, :])
    got_row = from_partner(send_row, "tile", 1)
    zero_col = jnp.zeros_like(got_col)
    zero_row = jnp.zeros_like(got_row)
    left_rim = jnp.where(col_bit == 1, got_col, zero_col)
    right_rim = jnp.where(col_bit == 0, got_col, zero_col)
    top_rim = jnp.where(row_bit == 1, got_row, zero_row)
    bottom_rim = jnp.where(row_bit == 0, got_row, zero_row)
    wide_pad = jnp.concatenate([left_rim[:, :, None], samples, right_rim[:, :, None]], axis=2)
    tall_pad = jnp.concatenate([top_rim[:, None, :], samples, bottom_rim[:, None, :]], axis=1)
    entries = jnp.arange(table_count, dtype=jnp.int32)
    table_grid = tables[:, :, None, None]

    def sample(step, carry):
        rgb, trans = carry
        wide = lax.dynamic_index_in_dim(wide_pad, step, 0, keepdims=False).astype(jnp.float32)
        tall = lax.dynamic_index_in_dim(tall_pad, step, 0, keepdims=False).astype(jnp.float32)
        cell_index = lax.dynamic_index_in_dim(cells, step, 0, keepdims=False)
        matches_cell = cell_index[None] == entries[:, None, None]
        cell_params = jnp.sum(jnp.where(matches_cell[None], table_grid, 0.0), axis=1)
        params = jnp.broadcast_to(cell_params[..., None], (param_count, height, cell_count, CELL))
        params = params.reshape(param_count, height, width)
        value = wide[:, 1:-1]
        grad_x = 0.5 * (wide[:, 2:] - wide[:, :-2])
        grad_y = 0.5 * (tall[2:, :] - tall[:-2, :])
        return light_sample(value, grad_x, grad_y, params, rgb, trans, inverse)

    start = (jnp.zeros((3, height, width), jnp.float32), jnp.ones((height, width), jnp.float32))
    rgb, trans = lax.fori_loop(0, depth_count, sample, start)
    partial_value = jnp.concatenate([rgb, (1.0 - trans)[None]], axis=0)
    piece_rows = height // ranks
    places = jnp.arange(ranks, dtype=jnp.int32)
    matches = brick_position[None, :] == places[:, None]
    rank_at = jnp.sum(jnp.where(matches, places[None, :], 0), axis=1)
    received = lax.all_to_all(partial_value, "depth", split_axis=1, concat_axis=0, tiled=True)
    stacked = received.reshape(ranks, 4, piece_rows, received.shape[2])
    ordered = jnp.take(stacked, rank_at, axis=0)
    image = composite(jnp.moveaxis(ordered, 0, 1))
    return image[:, None]


def fits(ranks, tiles, shape):
    height, width = shape[2], shape[3]
    even = ranks % 2 == 0 and tiles == 4 and height % ranks == 0
    return even and (height // ranks) % ROWS == 0 and width % (2 * LANES) == 0 and height % (2 * LANES) == 0


def solution(mesh):
    ranks = mesh.shape["depth"]
    tiles = mesh.shape["tile"]

    def program(volume, *rest):
        chosen = on_device
        if fits(ranks, tiles, volume.shape):
            chosen = functools.partial(fused_device, ranks, tiles)
        return jax.shard_map(
            chosen,
            mesh=mesh,
            in_specs=(P("depth", "tile", None, None), P("depth", "tile", None, None), P(), P(), P(), P(), P()),
            out_specs=P(None, "tile", "depth", None),
            check_vma=False,
        )(volume, *rest)

    return program
```

```python
import functools
import math
import jax
import jax.numpy as jnp
from jax import lax
from jax.experimental import pallas as pl
from jax.experimental.pallas import tpu as pltpu
from jax.sharding import PartitionSpec as P

CELL = 16
ROWS = 16
LANES = 128
RIM = 8
OCTAVES = 30.0
TOP_CODE = 65535.0
MID_CODE = 32768
SCALE = TOP_CODE / OCTAVES
LOG2E = 1.0 / math.log(2.0)
MESH = pl.DeviceIdType.MESH


def encode(value):
    code = jnp.log(value) * (-SCALE * LOG2E)
    code = jnp.minimum(jnp.maximum(code, 0.0), TOP_CODE)
    return ((code + 0.5).astype(jnp.int32) - MID_CODE).astype(jnp.int16)


def decode(code):
    steps = code.astype(jnp.int32).astype(jnp.float32)
    value = jnp.exp2((steps + float(MID_CODE)) * (-1.0 / SCALE))
    return jnp.where(steps >= TOP_CODE - MID_CODE, 0.0, value)


def march_kernel(
    ranks,
    tiles,
    position_ref,
    center_ref,
    width_ref,
    peak_ref,
    color_ref,
    index_ref,
    volume_ref,
    out_ref,
    padded,
    slab,
    order,
    half_eye,
    rim_pick,
    step_y,
    tables,
    turned,
    grad_y,
    cell_params,
    image_turned,
    outbox,
    inbox,
    load_sem,
    halo_send,
    halo_recv,
    send_sem,
    recv_sem,
    own_sem,
):
    depth_count, height, width = volume_ref.shape
    cells = index_ref.shape[1]
    span = half_eye.shape[0]
    window = step_y.shape[0]
    piece = height // ranks
    half = ranks // 2
    me = lax.axis_index("depth")
    tile = lax.axis_index("tile")
    col_bit = lax.rem(tile, 2)
    row_bit = lax.div(tile, 2)
    col_partner = tile + 1 - 2 * col_bit
    row_partner = lax.rem(tile + 2, tiles)
    side = lax.div(me, half)

    load = pltpu.make_async_copy(volume_ref, padded.at[:, pl.ds(ROWS, height), :], load_sem)
    load.start()

    barrier = pltpu.get_barrier_semaphore()

    def greet(apart, carry):
        other = lax.rem(me + apart, ranks)
        pl.semaphore_signal(barrier, inc=1, device_id=(other, tile), device_id_type=MESH)
        return carry

    lax.fori_loop(1, ranks, greet, 0)
    pl.semaphore_signal(barrier, inc=1, device_id=(me, col_partner), device_id_type=MESH)
    pl.semaphore_signal(barrier, inc=1, device_id=(me, row_partner), device_id_type=MESH)
    pl.semaphore_wait(barrier, ranks + 1)

    edge_row = pl.multiple_of((1 - row_bit) * (height - ROWS), ROWS)
    edge_col = pl.multiple_of((1 - col_bit) * (width - LANES), LANES)
    blank_row = pl.multiple_of(row_bit * (height + ROWS), ROWS)
    got_row = pl.multiple_of((1 - row_bit) * (height + ROWS), ROWS)
    send_row = pltpu.make_async_remote_copy(
        src_ref=volume_ref.at[:, pl.ds(edge_row, ROWS), :],
        dst_ref=padded.at[:, pl.ds(blank_row, ROWS), :],
        send_sem=halo_send.at[0],
        recv_sem=halo_recv.at[0],
        device_id=(me, row_partner),
        device_id_type=MESH,
    )
    send_row.start()
    send_col = pltpu.make_async_remote_copy(
        src_ref=volume_ref.at[:, :, pl.ds(edge_col, LANES)],
        dst_ref=slab,
        send_sem=halo_send.at[1],
        recv_sem=halo_recv.at[1],
        device_id=(me, col_partner),
        device_id_type=MESH,
    )
    send_col.start()
    padded[:, pl.ds(blank_row, ROWS), :] = jnp.zeros((depth_count, ROWS, width), jnp.bfloat16)

    for place in range(ranks):
        found = jnp.int32(0)
        for rank in range(ranks):
            found = jnp.where(position_ref[rank] == place, rank, found)
        order[place] = found

    def from_mask(mask, number):
        return jnp.where(mask, number, 0.0).astype(jnp.bfloat16)

    eye_row = lax.broadcasted_iota(jnp.int32, (span, span), 0)
    eye_col = lax.broadcasted_iota(jnp.int32, (span, span), 1)
    half_eye[...] = from_mask(eye_row == eye_col, 0.5)
    pick_row = lax.broadcasted_iota(jnp.int32, (ROWS, LANES), 0)
    pick_col = lax.broadcasted_iota(jnp.int32, (ROWS, LANES), 1)
    wanted_row = jnp.where(col_bit == 1, RIM - 1, RIM)
    wanted_col = jnp.where(col_bit == 1, LANES - 1, 0)
    rim_pick[...] = from_mask(jnp.logical_and(pick_row == wanted_row, pick_col == wanted_col), 0.5)
    window_row = lax.broadcasted_iota(jnp.int32, (window, LANES), 0)
    window_at = jnp.where(window_row < LANES, window_row, jnp.where(window_row < LANES + ROWS, window_row - LANES - ROWS, window_row - ROWS))
    lane_at = lax.broadcasted_iota(jnp.int32, (window, LANES), 1)
    plus = from_mask(window_at == lane_at + 1, 1.0)
    step_y[...] = plus - from_mask(window_at == lane_at - 1, 1.0)

    entries = center_ref.shape[1]
    gain = math.sqrt(0.5 * LOG2E) / width_ref[...]
    level = jnp.log(peak_ref[...] * (LOG2E / (depth_count * ranks))) * LOG2E
    tables[...] = jnp.zeros(tables.shape, jnp.float32)
    tables[0:1, 0:entries] = gain + gain
    tables[1:2, 0:entries] = gain * center_ref[...]
    tables[2:3, 0:entries] = level
    tables[3:6, 0:entries] = color_ref[...]

    load.wait()
    send_row.wait_send()
    send_col.wait_send()
    pltpu.make_async_remote_copy(
        src_ref=volume_ref.at[:, pl.ds(edge_row, ROWS), :],
        dst_ref=padded.at[:, pl.ds(got_row, ROWS), :],
        send_sem=halo_send.at[0],
        recv_sem=halo_recv.at[0],
        device_id=(me, row_partner),
        device_id_type=MESH,
    ).wait_recv()
    send_col.wait_recv()

    shade_x = 0.6 * math.sqrt(0.7)
    shade_y = 0.8 * math.sqrt(0.7)
    unit = math.gcd(piece, LANES)
    per_piece = piece // unit
    per_block = LANES // unit

    def post(segment):
        there = lax.div(segment, per_piece)
        rows = pl.multiple_of(segment * unit, ROWS)
        inside = pl.multiple_of(lax.rem(segment, per_piece) * unit, ROWS)
        return pltpu.make_async_remote_copy(
            src_ref=outbox.at[:, pl.ds(rows, unit), :],
            dst_ref=inbox.at[me, :, pl.ds(inside, unit), :],
            send_sem=send_sem.at[segment],
            recv_sem=recv_sem.at[me, lax.rem(segment, per_piece)],
            device_id=(there, tile),
            device_id_type=MESH,
        )

    blocks = height // LANES // 2
    transposed = (((1,), (1,)), ((), ()))

    def block(turn, carry):
        away = 1 - lax.div(turn, blocks)
        part = lax.rem(turn + me, blocks)
        area = lax.rem(side + away, 2)
        first = pl.multiple_of((area * blocks + part) * LANES, LANES)
        entry_rows = [jnp.broadcast_to(tables[p : p + 1, :], (cells, LANES)) for p in range(6)]

        def prepare(step, carry):
            index = index_ref[step, :, pl.ds(first, LANES)]
            for p in range(6):
                found = jnp.take_along_axis(entry_rows[p], index, axis=1, mode="promise_in_bounds")
                cell_params[step, p * cells : (p + 1) * cells, :] = found
            for left in range(0, width, span):
                cols = pl.ds(left, span)
                near = padded[step, pl.ds(pl.multiple_of(first + ROWS, ROWS), LANES), cols]
                above = padded[step, pl.ds(first, ROWS), cols]
                below = padded[step, pl.ds(pl.multiple_of(first + ROWS + LANES, ROWS), ROWS), cols]
                rows = jnp.concatenate([near, above, below], axis=0)
                flipped = lax.dot_general(half_eye[...], rows, transposed, preferred_element_type=jnp.float32)
                turned[step, RIM + left : RIM + left + span, :] = flipped[:, :LANES]
                grad_y[step, cols, :] = jnp.dot(
                    flipped.astype(jnp.bfloat16), step_y[...], preferred_element_type=jnp.float32
                )
            rim = slab[step, pl.ds(first, LANES), :]
            edges = lax.dot_general(rim_pick[...], rim, transposed, preferred_element_type=jnp.float32)
            turned[step, 0:RIM, :] = edges[:RIM]
            turned[step, RIM + width : 2 * RIM + width, :] = edges[RIM:]
            return carry

        lax.fori_loop(0, depth_count, prepare, 0, unroll=2)

        def column(cell, carry):
            top = pl.multiple_of(cell * CELL, CELL)

            def sample(step, carry):
                red, green, blue, trans = carry
                value = turned[step, pl.ds(top + RIM, CELL), :]
                gx = turned[step, pl.ds(top + RIM + 1, CELL), :] - turned[step, pl.ds(top + RIM - 1, CELL), :]
                gy = grad_y[step, pl.ds(top, CELL), :]

                def param(number):
                    row = cell_params[step, pl.ds(number * cells + cell, 1), :]
                    return jnp.broadcast_to(row, (CELL, LANES))

                energy = gx * gx + gy * gy
                facing = shade_x * gx + shade_y * gy
                base = 1.0 + energy
                rough = pl.reciprocal(base, approx=True)
                shade = 0.3 + facing * facing * (rough * (2.0 - base * rough))
                scaled = param(0) * value - param(1)
                keep = jnp.exp2(-(jnp.exp2(param(2) - scaled * scaled) * energy))
                weight = trans * (1.0 - keep) * shade
                return (
                    red + weight * param(3),
                    green + weight * param(4),
                    blue + weight * param(5),
                    trans * keep,
                )

            zero = jnp.zeros((CELL, LANES), jnp.float32)
            start = (zero, zero, zero, zero + 1.0)
            red, green, blue, trans = lax.fori_loop(0, depth_count, sample, start, unroll=True)
            for channel, image in enumerate((red, green, blue, 1.0 - trans)):
                image_turned[channel, pl.ds(top, CELL), :] = image
            return carry

        lax.fori_loop(0, cells, column, 0)

        for channel in range(4):
            for left in range(0, width, LANES):
                flat = image_turned[channel, left : left + LANES, :].T
                outbox[channel, pl.ds(first, LANES), left : left + LANES] = encode(flat)

        def dispatch(number, carry):
            segment = (area * blocks + part) * per_block + number

            @pl.when(lax.div(segment, per_piece) != me)
            def _():
                post(segment).start()

            return carry

        lax.fori_loop(0, per_block, dispatch, 0)
        return carry

    lax.fori_loop(0, 2 * blocks, block, 0)
    mine = outbox.at[:, pl.ds(pl.multiple_of(me * piece, ROWS), piece), :]
    own = pltpu.make_async_copy(mine, inbox.at[me], own_sem)
    own.start()
    own.wait()

    def settle(number, carry):
        there = lax.rem(me + 1 + lax.div(number, per_piece), ranks)
        inside = lax.rem(number, per_piece)
        post(there * per_piece + inside).wait_send()
        rows = pl.ds(pl.multiple_of(inside * unit, ROWS), unit)
        pltpu.make_async_remote_copy(
            src_ref=outbox.at[:, pl.ds(0, unit), :],
            dst_ref=inbox.at[there, :, rows, :],
            send_sem=send_sem.at[0],
            recv_sem=recv_sem.at[there, inside],
            device_id=(there, tile),
            device_id_type=MESH,
        ).wait_recv()
        return carry

    lax.fori_loop(0, (ranks - 1) * per_piece, settle, 0)

    def merge(part, carry):
        rows = pl.ds(pl.multiple_of(part * ROWS, ROWS), ROWS)
        for left in range(0, width, span):
            cols = pl.ds(left, span)

            def layer(place, images):
                rank = order[place]
                clear = 1.0 - images[3]
                return tuple(images[c] + clear * decode(inbox[rank, c, rows, cols]) for c in range(4))

            zero = jnp.zeros((ROWS, span), jnp.float32)
            images = lax.fori_loop(0, ranks, layer, (zero,) * 4, unroll=2)
            for c in range(4):
                out_ref[c, rows, cols] = images[c]
        return carry

    lax.fori_loop(0, piece // ROWS, merge, 0)


def fused_device(ranks, tiles, volume, table_index, brick_position, tf_center, tf_width, tf_peak, tf_color):
    samples = volume[:, 0]
    index = jnp.swapaxes(table_index[:, 0], 1, 2)
    depth_count, height, width = samples.shape
    piece = height // ranks
    cells = index.shape[1]
    image = pl.pallas_call(
        functools.partial(march_kernel, ranks, tiles),
        out_shape=jax.ShapeDtypeStruct((4, piece, width), jnp.float32),
        in_specs=[
            pl.BlockSpec(memory_space=pltpu.SMEM),
            pl.BlockSpec(memory_space=pltpu.VMEM),
            pl.BlockSpec(memory_space=pltpu.VMEM),
            pl.BlockSpec(memory_space=pltpu.VMEM),
            pl.BlockSpec(memory_space=pltpu.VMEM),
            pl.BlockSpec(memory_space=pltpu.VMEM),
            pl.BlockSpec(memory_space=pl.ANY),
        ],
        out_specs=pl.BlockSpec(memory_space=pltpu.VMEM),
        scratch_shapes=[
            pltpu.VMEM((depth_count, height + 2 * ROWS, width), jnp.bfloat16),
            pltpu.VMEM((depth_count, height, LANES), jnp.bfloat16),
            pltpu.SMEM((ranks,), jnp.int32),
            pltpu.VMEM((2 * LANES, 2 * LANES), jnp.bfloat16),
            pltpu.VMEM((ROWS, LANES), jnp.bfloat16),
            pltpu.VMEM((LANES + 2 * ROWS, LANES), jnp.bfloat16),
            pltpu.VMEM((8, LANES), jnp.float32),
            pltpu.VMEM((depth_count, width + 2 * RIM, LANES), jnp.float32),
            pltpu.VMEM((depth_count, width, LANES), jnp.float32),
            pltpu.VMEM((depth_count, 6 * cells, LANES), jnp.float32),
            pltpu.VMEM((4, width, LANES), jnp.float32),
            pltpu.VMEM((4, height, width), jnp.int16),
            pltpu.VMEM((ranks, 4, piece, width), jnp.int16),
            pltpu.SemaphoreType.DMA,
            pltpu.SemaphoreType.DMA((2,)),
            pltpu.SemaphoreType.DMA((2,)),
            pltpu.SemaphoreType.DMA((height // math.gcd(piece, LANES),)),
            pltpu.SemaphoreType.DMA((ranks, piece // math.gcd(piece, LANES))),
            pltpu.SemaphoreType.DMA,
        ],
        compiler_params=pltpu.CompilerParams(
            collective_id=0, has_side_effects=True, vmem_limit_bytes=56 * 1024 * 1024
        ),
    )(brick_position, tf_center[None], tf_width[None], tf_peak[None], tf_color, index, samples)
    return image[:, None]


def from_partner(value, axis, apart):
    return lax.ppermute(value, axis, [(i, i ^ 1 << apart) for i in range(lax.axis_size(axis))])


def light_sample(value, grad_x, grad_y, params, rgb, trans, inverse):
    energy = grad_x * grad_x + grad_y * grad_y
    facing = 0.6 * grad_x + 0.8 * grad_y
    shade = 0.3 + 0.7 * facing * facing / (1.0 + energy)
    scaled = (value - params[0]) / params[1]
    extinction = params[2] * jnp.exp(-0.5 * scaled * scaled) * energy * inverse
    keep = jnp.exp(-extinction)
    opacity = 1.0 - keep
    weight = trans * opacity
    rgb = rgb + weight[None] * params[3:6] * shade[None]
    trans = trans * keep
    return (rgb, trans)


def composite(layers):
    while layers.shape[1] > 1:
        front = layers[:, 0::2]
        back = layers[:, 1::2]
        layers = front + (1.0 - front[3:4]) * back
    return layers[:, 0]


def on_device(volume, table_index, brick_position, tf_center, tf_width, tf_peak, tf_color):
    tables = jnp.concatenate([tf_center[None], tf_width[None], tf_peak[None], tf_color], axis=0)
    samples = volume[:, 0]
    cells = table_index[:, 0]
    depth_count = samples.shape[0]
    height = samples.shape[1]
    width = samples.shape[2]
    cell_count = cells.shape[2]
    table_count = tables.shape[1]
    param_count = tables.shape[0]
    ranks = lax.axis_size("depth")
    inverse = 1.0 / (depth_count * ranks)
    tile_rank = lax.axis_index("tile")
    col_bit = tile_rank % 2
    row_bit = tile_rank // 2
    send_col = jnp.where(col_bit == 0, samples[:, :, width - 1], samples[:, :, 0])
    got_col = from_partner(send_col, "tile", 0)
    send_row = jnp.where(row_bit == 0, samples[:, height - 1, :], samples[:, 0, :])
    got_row = from_partner(send_row, "tile", 1)
    zero_col = jnp.zeros_like(got_col)
    zero_row = jnp.zeros_like(got_row)
    left_rim = jnp.where(col_bit == 1, got_col, zero_col)
    right_rim = jnp.where(col_bit == 0, got_col, zero_col)
    top_rim = jnp.where(row_bit == 1, got_row, zero_row)
    bottom_rim = jnp.where(row_bit == 0, got_row, zero_row)
    wide_pad = jnp.concatenate([left_rim[:, :, None], samples, right_rim[:, :, None]], axis=2)
    tall_pad = jnp.concatenate([top_rim[:, None, :], samples, bottom_rim[:, None, :]], axis=1)
    entries = jnp.arange(table_count, dtype=jnp.int32)
    table_grid = tables[:, :, None, None]

    def sample(step, carry):
        rgb, trans = carry
        wide = lax.dynamic_index_in_dim(wide_pad, step, 0, keepdims=False).astype(jnp.float32)
        tall = lax.dynamic_index_in_dim(tall_pad, step, 0, keepdims=False).astype(jnp.float32)
        cell_index = lax.dynamic_index_in_dim(cells, step, 0, keepdims=False)
        matches_cell = cell_index[None] == entries[:, None, None]
        cell_params = jnp.sum(jnp.where(matches_cell[None], table_grid, 0.0), axis=1)
        params = jnp.broadcast_to(cell_params[..., None], (param_count, height, cell_count, CELL))
        params = params.reshape(param_count, height, width)
        value = wide[:, 1:-1]
        grad_x = 0.5 * (wide[:, 2:] - wide[:, :-2])
        grad_y = 0.5 * (tall[2:, :] - tall[:-2, :])
        return light_sample(value, grad_x, grad_y, params, rgb, trans, inverse)

    start = (jnp.zeros((3, height, width), jnp.float32), jnp.ones((height, width), jnp.float32))
    rgb, trans = lax.fori_loop(0, depth_count, sample, start)
    partial_value = jnp.concatenate([rgb, (1.0 - trans)[None]], axis=0)
    piece_rows = height // ranks
    places = jnp.arange(ranks, dtype=jnp.int32)
    matches = brick_position[None, :] == places[:, None]
    rank_at = jnp.sum(jnp.where(matches, places[None, :], 0), axis=1)
    received = lax.all_to_all(partial_value, "depth", split_axis=1, concat_axis=0, tiled=True)
    stacked = received.reshape(ranks, 4, piece_rows, received.shape[2])
    ordered = jnp.take(stacked, rank_at, axis=0)
    image = composite(jnp.moveaxis(ordered, 0, 1))
    return image[:, None]


def fits(ranks, tiles, shape):
    height, width = shape[2], shape[3]
    even = ranks % 2 == 0 and tiles == 4 and height % ranks == 0
    return even and (height // ranks) % ROWS == 0 and width % (2 * LANES) == 0 and height % (2 * LANES) == 0


def solution(mesh):
    ranks = mesh.shape["depth"]
    tiles = mesh.shape["tile"]

    def program(volume, *rest):
        chosen = on_device
        if fits(ranks, tiles, volume.shape):
            chosen = functools.partial(fused_device, ranks, tiles)
        return jax.shard_map(
            chosen,
            mesh=mesh,
            in_specs=(P("depth", "tile", None, None), P("depth", "tile", None, None), P(), P(), P(), P(), P()),
            out_specs=P(None, "tile", "depth", None),
            check_vma=False,
        )(volume, *rest)

    return program
```

```python
import functools
import math
import jax
import jax.numpy as jnp
from jax import lax
from jax.experimental import pallas as pl
from jax.experimental.pallas import tpu as pltpu
from jax.sharding import PartitionSpec as P

CELL = 16
ROWS = 16
LANES = 128
RIM = 8
OCTAVES = 30.0
TOP_CODE = 65535.0
MID_CODE = 32768
SCALE = TOP_CODE / OCTAVES
LOG2E = 1.0 / math.log(2.0)
MESH = pl.DeviceIdType.MESH


def encode(value):
    code = jnp.log(value) * (-SCALE * LOG2E)
    code = jnp.minimum(jnp.maximum(code, 0.0), TOP_CODE)
    return ((code + 0.5).astype(jnp.int32) - MID_CODE).astype(jnp.int16)


def decode(code):
    steps = code.astype(jnp.int32).astype(jnp.float32)
    value = jnp.exp2((steps + float(MID_CODE)) * (-1.0 / SCALE))
    return jnp.where(steps >= TOP_CODE - MID_CODE, 0.0, value)


def march_kernel(
    ranks,
    tiles,
    position_ref,
    center_ref,
    width_ref,
    peak_ref,
    color_ref,
    index_ref,
    volume_ref,
    out_ref,
    padded,
    slab,
    order,
    half_eye,
    rim_pick,
    step_y,
    tables,
    turned,
    grad_y,
    cell_params,
    image_turned,
    outbox,
    inbox,
    load_sem,
    halo_send,
    halo_recv,
    send_sem,
    recv_sem,
    own_sem,
):
    depth_count, height, width = volume_ref.shape
    cells = index_ref.shape[1]
    span = half_eye.shape[0]
    window = step_y.shape[0]
    piece = height // ranks
    half = ranks // 2
    me = lax.axis_index("depth")
    tile = lax.axis_index("tile")
    col_bit = lax.rem(tile, 2)
    row_bit = lax.div(tile, 2)
    col_partner = tile + 1 - 2 * col_bit
    row_partner = lax.rem(tile + 2, tiles)
    side = lax.div(me, half)

    load = pltpu.make_async_copy(volume_ref, padded.at[:, pl.ds(ROWS, height), :], load_sem)
    load.start()

    barrier = pltpu.get_barrier_semaphore()

    def greet(apart, carry):
        other = lax.rem(me + apart, ranks)
        pl.semaphore_signal(barrier, inc=1, device_id=(other, tile), device_id_type=MESH)
        return carry

    lax.fori_loop(1, ranks, greet, 0)
    pl.semaphore_signal(barrier, inc=1, device_id=(me, col_partner), device_id_type=MESH)
    pl.semaphore_signal(barrier, inc=1, device_id=(me, row_partner), device_id_type=MESH)
    pl.semaphore_wait(barrier, ranks + 1)

    edge_row = pl.multiple_of((1 - row_bit) * (height - ROWS), ROWS)
    edge_col = pl.multiple_of((1 - col_bit) * (width - LANES), LANES)
    blank_row = pl.multiple_of(row_bit * (height + ROWS), ROWS)
    got_row = pl.multiple_of((1 - row_bit) * (height + ROWS), ROWS)
    send_row = pltpu.make_async_remote_copy(
        src_ref=volume_ref.at[:, pl.ds(edge_row, ROWS), :],
        dst_ref=padded.at[:, pl.ds(blank_row, ROWS), :],
        send_sem=halo_send.at[0],
        recv_sem=halo_recv.at[0],
        device_id=(me, row_partner),
        device_id_type=MESH,
    )
    send_row.start()
    send_col = pltpu.make_async_remote_copy(
        src_ref=volume_ref.at[:, :, pl.ds(edge_col, LANES)],
        dst_ref=slab,
        send_sem=halo_send.at[1],
        recv_sem=halo_recv.at[1],
        device_id=(me, col_partner),
        device_id_type=MESH,
    )
    send_col.start()
    padded[:, pl.ds(blank_row, ROWS), :] = jnp.zeros((depth_count, ROWS, width), jnp.bfloat16)

    for place in range(ranks):
        found = jnp.int32(0)
        for rank in range(ranks):
            found = jnp.where(position_ref[rank] == place, rank, found)
        order[place] = found

    def from_mask(mask, number):
        return jnp.where(mask, number, 0.0).astype(jnp.bfloat16)

    eye_row = lax.broadcasted_iota(jnp.int32, (span, span), 0)
    eye_col = lax.broadcasted_iota(jnp.int32, (span, span), 1)
    half_eye[...] = from_mask(eye_row == eye_col, 0.5)
    pick_row = lax.broadcasted_iota(jnp.int32, (ROWS, LANES), 0)
    pick_col = lax.broadcasted_iota(jnp.int32, (ROWS, LANES), 1)
    wanted_row = jnp.where(col_bit == 1, RIM - 1, RIM)
    wanted_col = jnp.where(col_bit == 1, LANES - 1, 0)
    rim_pick[...] = from_mask(jnp.logical_and(pick_row == wanted_row, pick_col == wanted_col), 0.5)
    window_row = lax.broadcasted_iota(jnp.int32, (window, LANES), 0)
    window_at = jnp.where(window_row < LANES, window_row, jnp.where(window_row < LANES + ROWS, window_row - LANES - ROWS, window_row - ROWS))
    lane_at = lax.broadcasted_iota(jnp.int32, (window, LANES), 1)
    plus = from_mask(window_at == lane_at + 1, 1.0)
    step_y[...] = plus - from_mask(window_at == lane_at - 1, 1.0)

    entries = center_ref.shape[1]
    gain = math.sqrt(0.5 * LOG2E) / width_ref[...]
    level = jnp.log(peak_ref[...] * (LOG2E / (depth_count * ranks))) * LOG2E
    tables[...] = jnp.zeros(tables.shape, jnp.float32)
    tables[0:1, 0:entries] = gain + gain
    tables[1:2, 0:entries] = gain * center_ref[...]
    tables[2:3, 0:entries] = level
    tables[3:6, 0:entries] = color_ref[...]

    load.wait()
    send_row.wait_send()
    send_col.wait_send()
    pltpu.make_async_remote_copy(
        src_ref=volume_ref.at[:, pl.ds(edge_row, ROWS), :],
        dst_ref=padded.at[:, pl.ds(got_row, ROWS), :],
        send_sem=halo_send.at[0],
        recv_sem=halo_recv.at[0],
        device_id=(me, row_partner),
        device_id_type=MESH,
    ).wait_recv()
    send_col.wait_recv()

    shade_x = 0.6 * math.sqrt(0.7)
    shade_y = 0.8 * math.sqrt(0.7)
    unit = math.gcd(piece, LANES)
    per_piece = piece // unit
    per_block = LANES // unit

    def post(segment, left):
        cols = pl.ds(left, span)
        slot = left // span
        there = lax.div(segment, per_piece)
        rows = pl.multiple_of(segment * unit, ROWS)
        inside = pl.multiple_of(lax.rem(segment, per_piece) * unit, ROWS)
        return pltpu.make_async_remote_copy(
            src_ref=outbox.at[:, pl.ds(rows, unit), cols],
            dst_ref=inbox.at[me, :, pl.ds(inside, unit), cols],
            send_sem=send_sem.at[segment, slot],
            recv_sem=recv_sem.at[me, lax.rem(segment, per_piece), slot],
            device_id=(there, tile),
            device_id_type=MESH,
        )

    blocks = height // LANES // 2
    transposed = (((1,), (1,)), ((), ()))

    def block(turn, carry):
        away = 1 - lax.div(turn, blocks)
        part = lax.rem(turn + me, blocks)
        area = lax.rem(side + away, 2)
        first = pl.multiple_of((area * blocks + part) * LANES, LANES)
        cells_half = span // CELL
        entry_rows = [jnp.broadcast_to(tables[p : p + 1, :], (cells_half, LANES)) for p in range(6)]

        def march(left):
            cols = pl.ds(left, span)
            first_cell = left // CELL

            def prepare(step, carry):
                index = index_ref[step, first_cell : first_cell + cells_half, pl.ds(first, LANES)]
                for p in range(6):
                    found = jnp.take_along_axis(entry_rows[p], index, axis=1, mode="promise_in_bounds")
                    begin = p * cells + first_cell
                    cell_params[step, begin : begin + cells_half, :] = found
                near = padded[step, pl.ds(pl.multiple_of(first + ROWS, ROWS), LANES), cols]
                above = padded[step, pl.ds(first, ROWS), cols]
                below = padded[step, pl.ds(pl.multiple_of(first + ROWS + LANES, ROWS), ROWS), cols]
                rows = jnp.concatenate([near, above, below], axis=0)
                flipped = lax.dot_general(half_eye[...], rows, transposed, preferred_element_type=jnp.float32)
                turned[step, RIM + left : RIM + left + span, :] = flipped[:, :LANES]
                grad_y[step, cols, :] = jnp.dot(
                    flipped.astype(jnp.bfloat16), step_y[...], preferred_element_type=jnp.float32
                )
                if left == 0:
                    rim = slab[step, pl.ds(first, LANES), :]
                    edges = lax.dot_general(rim_pick[...], rim, transposed, preferred_element_type=jnp.float32)
                    turned[step, 0:RIM, :] = edges[:RIM]
                    turned[step, RIM + width : 2 * RIM + width, :] = edges[RIM:]
                after = left + span
                if after < width:
                    beside = padded[
                        step, pl.ds(pl.multiple_of(first + ROWS, ROWS), LANES), after : after + LANES
                    ]
                    ahead = lax.dot_general(
                        half_eye[0:ROWS, 0:LANES], beside, transposed, preferred_element_type=jnp.float32
                    )
                    turned[step, RIM + after : 2 * RIM + after, :] = ahead[:RIM]
                return carry

            lax.fori_loop(0, depth_count, prepare, 0, unroll=4)

            def column(cell, carry):
                top = pl.multiple_of(cell * CELL, CELL)

                def sample(step, carry):
                    red, green, blue, trans = carry
                    value = turned[step, pl.ds(top + RIM, CELL), :]
                    gx = turned[step, pl.ds(top + RIM + 1, CELL), :] - turned[step, pl.ds(top + RIM - 1, CELL), :]
                    gy = grad_y[step, pl.ds(top, CELL), :]

                    def param(number):
                        row = cell_params[step, pl.ds(number * cells + cell, 1), :]
                        return jnp.broadcast_to(row, (CELL, LANES))

                    energy = gx * gx + gy * gy
                    facing = shade_x * gx + shade_y * gy
                    base = 1.0 + energy
                    rough = pl.reciprocal(base, approx=True)
                    shade = 0.3 + facing * facing * (rough * (2.0 - base * rough))
                    scaled = param(0) * value - param(1)
                    keep = jnp.exp2(-(jnp.exp2(param(2) - scaled * scaled) * energy))
                    weight = trans * (1.0 - keep) * shade
                    return (
                        red + weight * param(3),
                        green + weight * param(4),
                        blue + weight * param(5),
                        trans * keep,
                    )

                zero = jnp.zeros((CELL, LANES), jnp.float32)
                start = (zero, zero, zero, zero + 1.0)
                red, green, blue, trans = lax.fori_loop(0, depth_count, sample, start, unroll=True)
                for channel, image in enumerate((red, green, blue, 1.0 - trans)):
                    image_turned[channel, pl.ds(top, CELL), :] = image
                return carry

            lax.fori_loop(first_cell, first_cell + cells_half, column, 0)

            for channel in range(4):
                for at in range(left, left + span, LANES):
                    flat = image_turned[channel, at : at + LANES, :].T
                    outbox[channel, pl.ds(first, LANES), at : at + LANES] = encode(flat)

            def dispatch(number, carry):
                segment = (area * blocks + part) * per_block + number

                @pl.when(lax.div(segment, per_piece) != me)
                def _():
                    post(segment, left).start()

                return carry

            lax.fori_loop(0, per_block, dispatch, 0)

        for left in range(0, width, span):
            march(left)
        return carry

    lax.fori_loop(0, 2 * blocks, block, 0)
    mine = outbox.at[:, pl.ds(pl.multiple_of(me * piece, ROWS), piece), :]
    own = pltpu.make_async_copy(mine, inbox.at[me], own_sem)
    own.start()
    own.wait()

    def settle(number, carry):
        there = lax.rem(me + 1 + lax.div(number, per_piece), ranks)
        inside = lax.rem(number, per_piece)
        rows = pl.ds(pl.multiple_of(inside * unit, ROWS), unit)
        for left in range(0, width, span):
            post(there * per_piece + inside, left).wait_send()
            pltpu.make_async_remote_copy(
                src_ref=outbox.at[:, pl.ds(0, unit), pl.ds(left, span)],
                dst_ref=inbox.at[there, :, rows, pl.ds(left, span)],
                send_sem=send_sem.at[0, 0],
                recv_sem=recv_sem.at[there, inside, left // span],
                device_id=(there, tile),
                device_id_type=MESH,
            ).wait_recv()
        return carry

    lax.fori_loop(0, (ranks - 1) * per_piece, settle, 0)

    def merge(part, carry):
        rows = pl.ds(pl.multiple_of(part * ROWS, ROWS), ROWS)
        for left in range(0, width, span):
            cols = pl.ds(left, span)

            def layer(place, images):
                rank = order[place]
                clear = 1.0 - images[3]
                return tuple(images[c] + clear * decode(inbox[rank, c, rows, cols]) for c in range(4))

            zero = jnp.zeros((ROWS, span), jnp.float32)
            images = lax.fori_loop(0, ranks, layer, (zero,) * 4, unroll=2)
            for c in range(4):
                out_ref[c, rows, cols] = images[c]
        return carry

    lax.fori_loop(0, piece // ROWS, merge, 0)


def fused_device(ranks, tiles, volume, table_index, brick_position, tf_center, tf_width, tf_peak, tf_color):
    samples = volume[:, 0]
    index = jnp.swapaxes(table_index[:, 0], 1, 2)
    depth_count, height, width = samples.shape
    piece = height // ranks
    cells = index.shape[1]
    image = pl.pallas_call(
        functools.partial(march_kernel, ranks, tiles),
        out_shape=jax.ShapeDtypeStruct((4, piece, width), jnp.float32),
        in_specs=[
            pl.BlockSpec(memory_space=pltpu.SMEM),
            pl.BlockSpec(memory_space=pltpu.VMEM),
            pl.BlockSpec(memory_space=pltpu.VMEM),
            pl.BlockSpec(memory_space=pltpu.VMEM),
            pl.BlockSpec(memory_space=pltpu.VMEM),
            pl.BlockSpec(memory_space=pltpu.VMEM),
            pl.BlockSpec(memory_space=pl.ANY),
        ],
        out_specs=pl.BlockSpec(memory_space=pltpu.VMEM),
        scratch_shapes=[
            pltpu.VMEM((depth_count, height + 2 * ROWS, width), jnp.bfloat16),
            pltpu.VMEM((depth_count, height, LANES), jnp.bfloat16),
            pltpu.SMEM((ranks,), jnp.int32),
            pltpu.VMEM((2 * LANES, 2 * LANES), jnp.bfloat16),
            pltpu.VMEM((ROWS, LANES), jnp.bfloat16),
            pltpu.VMEM((LANES + 2 * ROWS, LANES), jnp.bfloat16),
            pltpu.VMEM((8, LANES), jnp.float32),
            pltpu.VMEM((depth_count, width + 2 * RIM, LANES), jnp.float32),
            pltpu.VMEM((depth_count, width, LANES), jnp.float32),
            pltpu.VMEM((depth_count, 6 * cells, LANES), jnp.float32),
            pltpu.VMEM((4, width, LANES), jnp.float32),
            pltpu.VMEM((4, height, width), jnp.int16),
            pltpu.VMEM((ranks, 4, piece, width), jnp.int16),
            pltpu.SemaphoreType.DMA,
            pltpu.SemaphoreType.DMA((2,)),
            pltpu.SemaphoreType.DMA((2,)),
            pltpu.SemaphoreType.DMA((height // math.gcd(piece, LANES), width // (2 * LANES))),
            pltpu.SemaphoreType.DMA((ranks, piece // math.gcd(piece, LANES), width // (2 * LANES))),
            pltpu.SemaphoreType.DMA,
        ],
        compiler_params=pltpu.CompilerParams(
            collective_id=0, has_side_effects=True, vmem_limit_bytes=56 * 1024 * 1024
        ),
    )(brick_position, tf_center[None], tf_width[None], tf_peak[None], tf_color, index, samples)
    return image[:, None]


def from_partner(value, axis, apart):
    return lax.ppermute(value, axis, [(i, i ^ 1 << apart) for i in range(lax.axis_size(axis))])


def light_sample(value, grad_x, grad_y, params, rgb, trans, inverse):
    energy = grad_x * grad_x + grad_y * grad_y
    facing = 0.6 * grad_x + 0.8 * grad_y
    shade = 0.3 + 0.7 * facing * facing / (1.0 + energy)
    scaled = (value - params[0]) / params[1]
    extinction = params[2] * jnp.exp(-0.5 * scaled * scaled) * energy * inverse
    keep = jnp.exp(-extinction)
    opacity = 1.0 - keep
    weight = trans * opacity
    rgb = rgb + weight[None] * params[3:6] * shade[None]
    trans = trans * keep
    return (rgb, trans)


def composite(layers):
    while layers.shape[1] > 1:
        front = layers[:, 0::2]
        back = layers[:, 1::2]
        layers = front + (1.0 - front[3:4]) * back
    return layers[:, 0]


def on_device(volume, table_index, brick_position, tf_center, tf_width, tf_peak, tf_color):
    tables = jnp.concatenate([tf_center[None], tf_width[None], tf_peak[None], tf_color], axis=0)
    samples = volume[:, 0]
    cells = table_index[:, 0]
    depth_count = samples.shape[0]
    height = samples.shape[1]
    width = samples.shape[2]
    cell_count = cells.shape[2]
    table_count = tables.shape[1]
    param_count = tables.shape[0]
    ranks = lax.axis_size("depth")
    inverse = 1.0 / (depth_count * ranks)
    tile_rank = lax.axis_index("tile")
    col_bit = tile_rank % 2
    row_bit = tile_rank // 2
    send_col = jnp.where(col_bit == 0, samples[:, :, width - 1], samples[:, :, 0])
    got_col = from_partner(send_col, "tile", 0)
    send_row = jnp.where(row_bit == 0, samples[:, height - 1, :], samples[:, 0, :])
    got_row = from_partner(send_row, "tile", 1)
    zero_col = jnp.zeros_like(got_col)
    zero_row = jnp.zeros_like(got_row)
    left_rim = jnp.where(col_bit == 1, got_col, zero_col)
    right_rim = jnp.where(col_bit == 0, got_col, zero_col)
    top_rim = jnp.where(row_bit == 1, got_row, zero_row)
    bottom_rim = jnp.where(row_bit == 0, got_row, zero_row)
    wide_pad = jnp.concatenate([left_rim[:, :, None], samples, right_rim[:, :, None]], axis=2)
    tall_pad = jnp.concatenate([top_rim[:, None, :], samples, bottom_rim[:, None, :]], axis=1)
    entries = jnp.arange(table_count, dtype=jnp.int32)
    table_grid = tables[:, :, None, None]

    def sample(step, carry):
        rgb, trans = carry
        wide = lax.dynamic_index_in_dim(wide_pad, step, 0, keepdims=False).astype(jnp.float32)
        tall = lax.dynamic_index_in_dim(tall_pad, step, 0, keepdims=False).astype(jnp.float32)
        cell_index = lax.dynamic_index_in_dim(cells, step, 0, keepdims=False)
        matches_cell = cell_index[None] == entries[:, None, None]
        cell_params = jnp.sum(jnp.where(matches_cell[None], table_grid, 0.0), axis=1)
        params = jnp.broadcast_to(cell_params[..., None], (param_count, height, cell_count, CELL))
        params = params.reshape(param_count, height, width)
        value = wide[:, 1:-1]
        grad_x = 0.5 * (wide[:, 2:] - wide[:, :-2])
        grad_y = 0.5 * (tall[2:, :] - tall[:-2, :])
        return light_sample(value, grad_x, grad_y, params, rgb, trans, inverse)

    start = (jnp.zeros((3, height, width), jnp.float32), jnp.ones((height, width), jnp.float32))
    rgb, trans = lax.fori_loop(0, depth_count, sample, start)
    partial_value = jnp.concatenate([rgb, (1.0 - trans)[None]], axis=0)
    piece_rows = height // ranks
    places = jnp.arange(ranks, dtype=jnp.int32)
    matches = brick_position[None, :] == places[:, None]
    rank_at = jnp.sum(jnp.where(matches, places[None, :], 0), axis=1)
    received = lax.all_to_all(partial_value, "depth", split_axis=1, concat_axis=0, tiled=True)
    stacked = received.reshape(ranks, 4, piece_rows, received.shape[2])
    ordered = jnp.take(stacked, rank_at, axis=0)
    image = composite(jnp.moveaxis(ordered, 0, 1))
    return image[:, None]


def fits(ranks, tiles, shape):
    height, width = shape[2], shape[3]
    even = ranks % 2 == 0 and tiles == 4 and height % ranks == 0
    return even and (height // ranks) % ROWS == 0 and width % (2 * LANES) == 0 and height % (2 * LANES) == 0


def solution(mesh):
    ranks = mesh.shape["depth"]
    tiles = mesh.shape["tile"]

    def program(volume, *rest):
        chosen = on_device
        if fits(ranks, tiles, volume.shape):
            chosen = functools.partial(fused_device, ranks, tiles)
        return jax.shard_map(
            chosen,
            mesh=mesh,
            in_specs=(P("depth", "tile", None, None), P("depth", "tile", None, None), P(), P(), P(), P(), P()),
            out_specs=P(None, "tile", "depth", None),
            check_vma=False,
        )(volume, *rest)

    return program
```

```python
import functools
import math
import jax
import jax.numpy as jnp
from jax import lax
from jax.experimental import pallas as pl
from jax.experimental.pallas import tpu as pltpu
from jax.sharding import PartitionSpec as P

CELL = 16
ROWS = 16
LANES = 128
RIM = 8
OCTAVES = 30.0
TOP_CODE = 65535.0
MID_CODE = 32768
SCALE = TOP_CODE / OCTAVES
LOG2E = 1.0 / math.log(2.0)
MESH = pl.DeviceIdType.MESH


def encode(value):
    code = jnp.log(value) * (-SCALE * LOG2E)
    code = jnp.minimum(jnp.maximum(code, 0.0), TOP_CODE)
    return ((code + 0.5).astype(jnp.int32) - MID_CODE).astype(jnp.int16)


def decode(code):
    steps = code.astype(jnp.int32).astype(jnp.float32)
    value = jnp.exp2((steps + float(MID_CODE)) * (-1.0 / SCALE))
    return jnp.where(steps >= TOP_CODE - MID_CODE, 0.0, value)


def march_kernel(
    ranks,
    tiles,
    position_ref,
    center_ref,
    width_ref,
    peak_ref,
    color_ref,
    index_ref,
    volume_ref,
    out_ref,
    padded,
    slab,
    order,
    half_eye,
    rim_pick,
    inner_pick,
    step_y,
    tables,
    turned_parts,
    grad_parts,
    param_parts,
    image_turned,
    outbox,
    inbox,
    load_sem,
    halo_send,
    halo_recv,
    send_sem,
    recv_sem,
    own_sem,
):
    depth_count, height, width = volume_ref.shape
    cells = index_ref.shape[1]
    span = half_eye.shape[0]
    window = step_y.shape[0]
    piece = height // ranks
    half = ranks // 2
    me = lax.axis_index("depth")
    tile = lax.axis_index("tile")
    col_bit = lax.rem(tile, 2)
    row_bit = lax.div(tile, 2)
    col_partner = tile + 1 - 2 * col_bit
    row_partner = lax.rem(tile + 2, tiles)
    side = lax.div(me, half)

    load = pltpu.make_async_copy(volume_ref, padded.at[:, pl.ds(ROWS, height), :], load_sem)
    load.start()

    barrier = pltpu.get_barrier_semaphore()

    def greet(apart, carry):
        other = lax.rem(me + apart, ranks)
        pl.semaphore_signal(barrier, inc=1, device_id=(other, tile), device_id_type=MESH)
        return carry

    lax.fori_loop(1, ranks, greet, 0)
    pl.semaphore_signal(barrier, inc=1, device_id=(me, col_partner), device_id_type=MESH)
    pl.semaphore_signal(barrier, inc=1, device_id=(me, row_partner), device_id_type=MESH)
    pl.semaphore_wait(barrier, ranks + 1)

    edge_row = pl.multiple_of((1 - row_bit) * (height - ROWS), ROWS)
    edge_col = pl.multiple_of((1 - col_bit) * (width - LANES), LANES)
    blank_row = pl.multiple_of(row_bit * (height + ROWS), ROWS)
    got_row = pl.multiple_of((1 - row_bit) * (height + ROWS), ROWS)
    send_row = pltpu.make_async_remote_copy(
        src_ref=volume_ref.at[:, pl.ds(edge_row, ROWS), :],
        dst_ref=padded.at[:, pl.ds(blank_row, ROWS), :],
        send_sem=halo_send.at[0],
        recv_sem=halo_recv.at[0],
        device_id=(me, row_partner),
        device_id_type=MESH,
    )
    send_row.start()
    send_col = pltpu.make_async_remote_copy(
        src_ref=volume_ref.at[:, :, pl.ds(edge_col, LANES)],
        dst_ref=slab,
        send_sem=halo_send.at[1],
        recv_sem=halo_recv.at[1],
        device_id=(me, col_partner),
        device_id_type=MESH,
    )
    send_col.start()
    padded[:, pl.ds(blank_row, ROWS), :] = jnp.zeros((depth_count, ROWS, width), jnp.bfloat16)

    for place in range(ranks):
        found = jnp.int32(0)
        for rank in range(ranks):
            found = jnp.where(position_ref[rank] == place, rank, found)
        order[place] = found

    def from_mask(mask, number):
        return jnp.where(mask, number, 0.0).astype(jnp.bfloat16)

    eye_row = lax.broadcasted_iota(jnp.int32, (span, span), 0)
    eye_col = lax.broadcasted_iota(jnp.int32, (span, span), 1)
    half_eye[...] = from_mask(eye_row == eye_col, 0.5)
    pick_row = lax.broadcasted_iota(jnp.int32, (ROWS, LANES), 0)
    pick_col = lax.broadcasted_iota(jnp.int32, (ROWS, LANES), 1)
    wanted_left = jnp.logical_and(pick_row == RIM - 1, pick_col == LANES - 1)
    wanted_right = jnp.logical_and(pick_row == RIM, pick_col == 0)
    inner_pick[...] = from_mask(jnp.logical_or(wanted_left, wanted_right), 0.5)
    wanted_row = jnp.where(col_bit == 1, RIM - 1, RIM)
    wanted_col = jnp.where(col_bit == 1, LANES - 1, 0)
    rim_pick[...] = from_mask(jnp.logical_and(pick_row == wanted_row, pick_col == wanted_col), 0.5)
    window_row = lax.broadcasted_iota(jnp.int32, (window, LANES), 0)
    window_at = jnp.where(window_row < LANES, window_row, jnp.where(window_row < LANES + ROWS, window_row - LANES - ROWS, window_row - ROWS))
    lane_at = lax.broadcasted_iota(jnp.int32, (window, LANES), 1)
    plus = from_mask(window_at == lane_at + 1, 1.0)
    step_y[...] = plus - from_mask(window_at == lane_at - 1, 1.0)

    entries = center_ref.shape[1]
    gain = math.sqrt(0.5 * LOG2E) / width_ref[...]
    level = jnp.log(peak_ref[...] * (LOG2E / (depth_count * ranks))) * LOG2E
    tables[...] = jnp.zeros(tables.shape, jnp.float32)
    tables[0:1, 0:entries] = gain + gain
    tables[1:2, 0:entries] = gain * center_ref[...]
    tables[2:3, 0:entries] = level
    tables[3:6, 0:entries] = color_ref[...]

    load.wait()
    send_row.wait_send()
    send_col.wait_send()
    pltpu.make_async_remote_copy(
        src_ref=volume_ref.at[:, pl.ds(edge_row, ROWS), :],
        dst_ref=padded.at[:, pl.ds(got_row, ROWS), :],
        send_sem=halo_send.at[0],
        recv_sem=halo_recv.at[0],
        device_id=(me, row_partner),
        device_id_type=MESH,
    ).wait_recv()
    send_col.wait_recv()

    shade_x = 0.6 * math.sqrt(0.7)
    shade_y = 0.8 * math.sqrt(0.7)
    unit = math.gcd(piece, LANES)
    per_piece = piece // unit
    per_block = LANES // unit

    def post(segment, left):
        cols = pl.ds(left, span)
        slot = left // span
        there = lax.div(segment, per_piece)
        rows = pl.multiple_of(segment * unit, ROWS)
        inside = pl.multiple_of(lax.rem(segment, per_piece) * unit, ROWS)
        return pltpu.make_async_remote_copy(
            src_ref=outbox.at[:, pl.ds(rows, unit), cols],
            dst_ref=inbox.at[me, :, pl.ds(inside, unit), cols],
            send_sem=send_sem.at[segment, slot],
            recv_sem=recv_sem.at[me, lax.rem(segment, per_piece), slot],
            device_id=(there, tile),
            device_id_type=MESH,
        )

    blocks = height // LANES // 2
    transposed = (((1,), (1,)), ((), ()))

    parts = width // span
    cells_part = span // CELL
    laps = math.gcd(depth_count, cells_part)

    def spot(turn):
        area = lax.rem(side + 1 - lax.div(turn, blocks), 2)
        return area * blocks + lax.rem(turn + me, blocks)

    def prepare(part, first, step):
        left = part * span
        cols = pl.ds(left, span)
        turned = turned_parts[part]
        middle = pl.ds(pl.multiple_of(first + ROWS, ROWS), LANES)
        index = index_ref[step, part * cells_part : (part + 1) * cells_part, pl.ds(first, LANES)]
        for p in range(6):
            entries_wide = jnp.broadcast_to(tables[p : p + 1, :], (cells_part, LANES))
            found = jnp.take_along_axis(entries_wide, index, axis=1, mode="promise_in_bounds")
            param_parts[part][step, p * cells_part : (p + 1) * cells_part, :] = found
        near = padded[step, middle, cols]
        above = padded[step, pl.ds(first, ROWS), cols]
        below = padded[step, pl.ds(pl.multiple_of(first + ROWS + LANES, ROWS), ROWS), cols]
        rows = jnp.concatenate([near, above, below], axis=0)
        flipped = lax.dot_general(half_eye[...], rows, transposed, preferred_element_type=jnp.float32)
        turned[step, RIM : RIM + span, :] = flipped[:, :LANES]
        grad_parts[part][step] = jnp.dot(
            flipped.astype(jnp.bfloat16), step_y[...], preferred_element_type=jnp.float32
        )

        def edges(pick, beside):
            return lax.dot_general(pick[...], beside, transposed, preferred_element_type=jnp.float32)

        rim = slab[step, pl.ds(first, LANES), :]
        before = edges(rim_pick, rim) if part == 0 else edges(inner_pick, padded[step, middle, left - LANES : left])
        after = left + span
        if part == parts - 1:
            behind = edges(rim_pick, rim)
        else:
            behind = edges(inner_pick, padded[step, middle, after : after + LANES])
        turned[step, 0:RIM, :] = before[:RIM]
        turned[step, RIM + span : 2 * RIM + span, :] = behind[RIM:]

    def march(part, cell):
        turned = turned_parts[part]
        grad_y = grad_parts[part]
        params = param_parts[part]
        top = pl.multiple_of(cell * CELL, CELL)

        def sample(step, carry):
            red, green, blue, trans = carry
            value = turned[step, pl.ds(top + RIM, CELL), :]
            gx = turned[step, pl.ds(top + RIM + 1, CELL), :] - turned[step, pl.ds(top + RIM - 1, CELL), :]
            gy = grad_y[step, pl.ds(top, CELL), :]

            def param(number):
                row = params[step, pl.ds(number * cells_part + cell, 1), :]
                return jnp.broadcast_to(row, (CELL, LANES))

            energy = gx * gx + gy * gy
            facing = shade_x * gx + shade_y * gy
            base = 1.0 + energy
            rough = pl.reciprocal(base, approx=True)
            shade = 0.3 + facing * facing * (rough * (2.0 - base * rough))
            scaled = param(0) * value - param(1)
            keep = jnp.exp2(-(jnp.exp2(param(2) - scaled * scaled) * energy))
            weight = trans * (1.0 - keep) * shade
            return (
                red + weight * param(3),
                green + weight * param(4),
                blue + weight * param(5),
                trans * keep,
            )

        zero = jnp.zeros((CELL, LANES), jnp.float32)
        start = (zero, zero, zero, zero + 1.0)
        red, green, blue, trans = lax.fori_loop(0, depth_count, sample, start, unroll=True)
        for channel, image in enumerate((red, green, blue, 1.0 - trans)):
            image_turned[channel, pl.ds(top, CELL), :] = image

    def block(turn, carry):
        place = spot(turn)
        first = pl.multiple_of(place * LANES, LANES)
        later = pl.multiple_of(spot(lax.rem(turn + 1, 2 * blocks)) * LANES, LANES)

        for part in range(parts):
            following = (part + 1) % parts
            upcoming = later if following == 0 else first

            def lap(number, carry):
                for extra in range(depth_count // laps):
                    prepare(following, upcoming, number * (depth_count // laps) + extra)
                for extra in range(cells_part // laps):
                    march(part, number * (cells_part // laps) + extra)
                return carry

            lax.fori_loop(0, laps, lap, 0)

            left = part * span
            for channel in range(4):
                for at in range(0, span, LANES):
                    flat = image_turned[channel, at : at + LANES, :].T
                    outbox[channel, pl.ds(first, LANES), left + at : left + at + LANES] = encode(flat)

            def dispatch(number, carry):
                segment = place * per_block + number

                @pl.when(lax.div(segment, per_piece) != me)
                def _():
                    post(segment, left).start()

                return carry

            lax.fori_loop(0, per_block, dispatch, 0)
        return carry

    opening = pl.multiple_of(spot(0) * LANES, LANES)

    def begin(step, carry):
        prepare(0, opening, step)
        return carry

    lax.fori_loop(0, depth_count, begin, 0, unroll=4)
    lax.fori_loop(0, 2 * blocks, block, 0)
    mine = outbox.at[:, pl.ds(pl.multiple_of(me * piece, ROWS), piece), :]
    own = pltpu.make_async_copy(mine, inbox.at[me], own_sem)
    own.start()
    own.wait()

    def settle(number, carry):
        there = lax.rem(me + 1 + lax.div(number, per_piece), ranks)
        inside = lax.rem(number, per_piece)
        rows = pl.ds(pl.multiple_of(inside * unit, ROWS), unit)
        for left in range(0, width, span):
            post(there * per_piece + inside, left).wait_send()
            pltpu.make_async_remote_copy(
                src_ref=outbox.at[:, pl.ds(0, unit), pl.ds(left, span)],
                dst_ref=inbox.at[there, :, rows, pl.ds(left, span)],
                send_sem=send_sem.at[0, 0],
                recv_sem=recv_sem.at[there, inside, left // span],
                device_id=(there, tile),
                device_id_type=MESH,
            ).wait_recv()
        return carry

    lax.fori_loop(0, (ranks - 1) * per_piece, settle, 0)

    def merge(part, carry):
        rows = pl.ds(pl.multiple_of(part * ROWS, ROWS), ROWS)
        for left in range(0, width, span):
            cols = pl.ds(left, span)

            def layer(place, images):
                rank = order[place]
                clear = 1.0 - images[3]
                return tuple(images[c] + clear * decode(inbox[rank, c, rows, cols]) for c in range(4))

            zero = jnp.zeros((ROWS, span), jnp.float32)
            images = lax.fori_loop(0, ranks, layer, (zero,) * 4, unroll=2)
            for c in range(4):
                out_ref[c, rows, cols] = images[c]
        return carry

    lax.fori_loop(0, piece // ROWS, merge, 0)


def fused_device(ranks, tiles, volume, table_index, brick_position, tf_center, tf_width, tf_peak, tf_color):
    samples = volume[:, 0]
    index = jnp.swapaxes(table_index[:, 0], 1, 2)
    depth_count, height, width = samples.shape
    piece = height // ranks
    cells = index.shape[1]
    span = 2 * LANES
    parts = width // span
    image = pl.pallas_call(
        functools.partial(march_kernel, ranks, tiles),
        out_shape=jax.ShapeDtypeStruct((4, piece, width), jnp.float32),
        in_specs=[
            pl.BlockSpec(memory_space=pltpu.SMEM),
            pl.BlockSpec(memory_space=pltpu.VMEM),
            pl.BlockSpec(memory_space=pltpu.VMEM),
            pl.BlockSpec(memory_space=pltpu.VMEM),
            pl.BlockSpec(memory_space=pltpu.VMEM),
            pl.BlockSpec(memory_space=pltpu.VMEM),
            pl.BlockSpec(memory_space=pl.ANY),
        ],
        out_specs=pl.BlockSpec(memory_space=pltpu.VMEM),
        scratch_shapes=[
            pltpu.VMEM((depth_count, height + 2 * ROWS, width), jnp.bfloat16),
            pltpu.VMEM((depth_count, height, LANES), jnp.bfloat16),
            pltpu.SMEM((ranks,), jnp.int32),
            pltpu.VMEM((2 * LANES, 2 * LANES), jnp.bfloat16),
            pltpu.VMEM((ROWS, LANES), jnp.bfloat16),
            pltpu.VMEM((ROWS, LANES), jnp.bfloat16),
            pltpu.VMEM((LANES + 2 * ROWS, LANES), jnp.bfloat16),
            pltpu.VMEM((8, LANES), jnp.float32),
            [pltpu.VMEM((depth_count, span + 2 * RIM, LANES), jnp.float32)] * parts,
            [pltpu.VMEM((depth_count, span, LANES), jnp.float32)] * parts,
            [pltpu.VMEM((depth_count, 6 * (span // CELL), LANES), jnp.float32)] * parts,
            pltpu.VMEM((4, span, LANES), jnp.float32),
            pltpu.VMEM((4, height, width), jnp.int16),
            pltpu.VMEM((ranks, 4, piece, width), jnp.int16),
            pltpu.SemaphoreType.DMA,
            pltpu.SemaphoreType.DMA((2,)),
            pltpu.SemaphoreType.DMA((2,)),
            pltpu.SemaphoreType.DMA((height // math.gcd(piece, LANES), width // (2 * LANES))),
            pltpu.SemaphoreType.DMA((ranks, piece // math.gcd(piece, LANES), width // (2 * LANES))),
            pltpu.SemaphoreType.DMA,
        ],
        compiler_params=pltpu.CompilerParams(
            collective_id=0, has_side_effects=True, vmem_limit_bytes=56 * 1024 * 1024
        ),
    )(brick_position, tf_center[None], tf_width[None], tf_peak[None], tf_color, index, samples)
    return image[:, None]


def from_partner(value, axis, apart):
    return lax.ppermute(value, axis, [(i, i ^ 1 << apart) for i in range(lax.axis_size(axis))])


def light_sample(value, grad_x, grad_y, params, rgb, trans, inverse):
    energy = grad_x * grad_x + grad_y * grad_y
    facing = 0.6 * grad_x + 0.8 * grad_y
    shade = 0.3 + 0.7 * facing * facing / (1.0 + energy)
    scaled = (value - params[0]) / params[1]
    extinction = params[2] * jnp.exp(-0.5 * scaled * scaled) * energy * inverse
    keep = jnp.exp(-extinction)
    opacity = 1.0 - keep
    weight = trans * opacity
    rgb = rgb + weight[None] * params[3:6] * shade[None]
    trans = trans * keep
    return (rgb, trans)


def composite(layers):
    while layers.shape[1] > 1:
        front = layers[:, 0::2]
        back = layers[:, 1::2]
        layers = front + (1.0 - front[3:4]) * back
    return layers[:, 0]


def on_device(volume, table_index, brick_position, tf_center, tf_width, tf_peak, tf_color):
    tables = jnp.concatenate([tf_center[None], tf_width[None], tf_peak[None], tf_color], axis=0)
    samples = volume[:, 0]
    cells = table_index[:, 0]
    depth_count = samples.shape[0]
    height = samples.shape[1]
    width = samples.shape[2]
    cell_count = cells.shape[2]
    table_count = tables.shape[1]
    param_count = tables.shape[0]
    ranks = lax.axis_size("depth")
    inverse = 1.0 / (depth_count * ranks)
    tile_rank = lax.axis_index("tile")
    col_bit = tile_rank % 2
    row_bit = tile_rank // 2
    send_col = jnp.where(col_bit == 0, samples[:, :, width - 1], samples[:, :, 0])
    got_col = from_partner(send_col, "tile", 0)
    send_row = jnp.where(row_bit == 0, samples[:, height - 1, :], samples[:, 0, :])
    got_row = from_partner(send_row, "tile", 1)
    zero_col = jnp.zeros_like(got_col)
    zero_row = jnp.zeros_like(got_row)
    left_rim = jnp.where(col_bit == 1, got_col, zero_col)
    right_rim = jnp.where(col_bit == 0, got_col, zero_col)
    top_rim = jnp.where(row_bit == 1, got_row, zero_row)
    bottom_rim = jnp.where(row_bit == 0, got_row, zero_row)
    wide_pad = jnp.concatenate([left_rim[:, :, None], samples, right_rim[:, :, None]], axis=2)
    tall_pad = jnp.concatenate([top_rim[:, None, :], samples, bottom_rim[:, None, :]], axis=1)
    entries = jnp.arange(table_count, dtype=jnp.int32)
    table_grid = tables[:, :, None, None]

    def sample(step, carry):
        rgb, trans = carry
        wide = lax.dynamic_index_in_dim(wide_pad, step, 0, keepdims=False).astype(jnp.float32)
        tall = lax.dynamic_index_in_dim(tall_pad, step, 0, keepdims=False).astype(jnp.float32)
        cell_index = lax.dynamic_index_in_dim(cells, step, 0, keepdims=False)
        matches_cell = cell_index[None] == entries[:, None, None]
        cell_params = jnp.sum(jnp.where(matches_cell[None], table_grid, 0.0), axis=1)
        params = jnp.broadcast_to(cell_params[..., None], (param_count, height, cell_count, CELL))
        params = params.reshape(param_count, height, width)
        value = wide[:, 1:-1]
        grad_x = 0.5 * (wide[:, 2:] - wide[:, :-2])
        grad_y = 0.5 * (tall[2:, :] - tall[:-2, :])
        return light_sample(value, grad_x, grad_y, params, rgb, trans, inverse)

    start = (jnp.zeros((3, height, width), jnp.float32), jnp.ones((height, width), jnp.float32))
    rgb, trans = lax.fori_loop(0, depth_count, sample, start)
    partial_value = jnp.concatenate([rgb, (1.0 - trans)[None]], axis=0)
    piece_rows = height // ranks
    places = jnp.arange(ranks, dtype=jnp.int32)
    matches = brick_position[None, :] == places[:, None]
    rank_at = jnp.sum(jnp.where(matches, places[None, :], 0), axis=1)
    received = lax.all_to_all(partial_value, "depth", split_axis=1, concat_axis=0, tiled=True)
    stacked = received.reshape(ranks, 4, piece_rows, received.shape[2])
    ordered = jnp.take(stacked, rank_at, axis=0)
    image = composite(jnp.moveaxis(ordered, 0, 1))
    return image[:, None]


def fits(ranks, tiles, shape):
    height, width = shape[2], shape[3]
    even = ranks % 2 == 0 and tiles == 4 and height % ranks == 0
    return even and (height // ranks) % ROWS == 0 and width % (2 * LANES) == 0 and width > 2 * LANES and height % (2 * LANES) == 0


def solution(mesh):
    ranks = mesh.shape["depth"]
    tiles = mesh.shape["tile"]

    def program(volume, *rest):
        chosen = on_device
        if fits(ranks, tiles, volume.shape):
            chosen = functools.partial(fused_device, ranks, tiles)
        return jax.shard_map(
            chosen,
            mesh=mesh,
            in_specs=(P("depth", "tile", None, None), P("depth", "tile", None, None), P(), P(), P(), P(), P()),
            out_specs=P(None, "tile", "depth", None),
            check_vma=False,
        )(volume, *rest)

    return program
```

```python
import functools
import math
import jax
import jax.numpy as jnp
from jax import lax
from jax.experimental import pallas as pl
from jax.experimental.pallas import tpu as pltpu
from jax.sharding import PartitionSpec as P

CELL = 16
ROWS = 16
LANES = 128
RIM = 8
OCTAVES = 30.0
TOP_CODE = 65535.0
MID_CODE = 32768
SCALE = TOP_CODE / OCTAVES
LOG2E = 1.0 / math.log(2.0)
MESH = pl.DeviceIdType.MESH


def encode(value):
    code = jnp.log(value) * (-SCALE * LOG2E)
    code = jnp.minimum(jnp.maximum(code, 0.0), TOP_CODE)
    return ((code + 0.5).astype(jnp.int32) - MID_CODE).astype(jnp.int16)


def decode(code):
    steps = code.astype(jnp.int32).astype(jnp.float32)
    value = jnp.exp((steps + float(MID_CODE)) * (-1.0 / (SCALE * LOG2E)))
    return jnp.where(steps >= TOP_CODE - MID_CODE, 0.0, value)


def march_kernel(
    ranks,
    tiles,
    position_ref,
    center_ref,
    width_ref,
    peak_ref,
    color_ref,
    index_ref,
    volume_ref,
    out_ref,
    padded,
    slab,
    order,
    half_eye,
    rim_pick,
    step_y,
    tables,
    turned,
    grad_y,
    cell_params,
    image_turned,
    outbox,
    inbox,
    load_sem,
    halo_send,
    halo_recv,
    send_sem,
    recv_sem,
    own_sem,
):
    depth_count, height, width = volume_ref.shape
    cells = index_ref.shape[1]
    span = half_eye.shape[0]
    window = step_y.shape[0]
    piece = height // ranks
    half = ranks // 2
    me = lax.axis_index("depth")
    tile = lax.axis_index("tile")
    col_bit = lax.rem(tile, 2)
    row_bit = lax.div(tile, 2)
    col_partner = tile + 1 - 2 * col_bit
    row_partner = lax.rem(tile + 2, tiles)
    side = lax.div(me, half)

    load = pltpu.make_async_copy(volume_ref, padded.at[:, pl.ds(ROWS, height), :], load_sem)
    load.start()

    barrier = pltpu.get_barrier_semaphore()

    def greet(apart, carry):
        other = lax.rem(me + apart, ranks)
        pl.semaphore_signal(barrier, inc=1, device_id=(other, tile), device_id_type=MESH)
        return carry

    lax.fori_loop(1, ranks, greet, 0)
    pl.semaphore_signal(barrier, inc=1, device_id=(me, col_partner), device_id_type=MESH)
    pl.semaphore_signal(barrier, inc=1, device_id=(me, row_partner), device_id_type=MESH)
    pl.semaphore_wait(barrier, ranks + 1)

    edge_row = pl.multiple_of((1 - row_bit) * (height - ROWS), ROWS)
    edge_col = pl.multiple_of((1 - col_bit) * (width - LANES), LANES)
    blank_row = pl.multiple_of(row_bit * (height + ROWS), ROWS)
    got_row = pl.multiple_of((1 - row_bit) * (height + ROWS), ROWS)
    send_row = pltpu.make_async_remote_copy(
        src_ref=volume_ref.at[:, pl.ds(edge_row, ROWS), :],
        dst_ref=padded.at[:, pl.ds(blank_row, ROWS), :],
        send_sem=halo_send.at[0],
        recv_sem=halo_recv.at[0],
        device_id=(me, row_partner),
        device_id_type=MESH,
    )
    send_row.start()
    send_col = pltpu.make_async_remote_copy(
        src_ref=volume_ref.at[:, :, pl.ds(edge_col, LANES)],
        dst_ref=slab,
        send_sem=halo_send.at[1],
        recv_sem=halo_recv.at[1],
        device_id=(me, col_partner),
        device_id_type=MESH,
    )
    send_col.start()
    padded[:, pl.ds(blank_row, ROWS), :] = jnp.zeros((depth_count, ROWS, width), jnp.bfloat16)

    for place in range(ranks):
        found = jnp.int32(0)
        for rank in range(ranks):
            found = jnp.where(position_ref[rank] == place, rank, found)
        order[place] = found

    def from_mask(mask, number):
        return jnp.where(mask, number, 0.0).astype(jnp.bfloat16)

    eye_row = lax.broadcasted_iota(jnp.int32, (span, span), 0)
    eye_col = lax.broadcasted_iota(jnp.int32, (span, span), 1)
    half_eye[...] = from_mask(eye_row == eye_col, 0.5)
    pick_row = lax.broadcasted_iota(jnp.int32, (ROWS, LANES), 0)
    pick_col = lax.broadcasted_iota(jnp.int32, (ROWS, LANES), 1)
    wanted_row = jnp.where(col_bit == 1, RIM - 1, RIM)
    wanted_col = jnp.where(col_bit == 1, LANES - 1, 0)
    rim_pick[...] = from_mask(jnp.logical_and(pick_row == wanted_row, pick_col == wanted_col), 0.5)
    window_row = lax.broadcasted_iota(jnp.int32, (window, LANES), 0)
    window_at = jnp.where(window_row < LANES, window_row, jnp.where(window_row < LANES + ROWS, window_row - LANES - ROWS, window_row - ROWS))
    lane_at = lax.broadcasted_iota(jnp.int32, (window, LANES), 1)
    plus = from_mask(window_at == lane_at + 1, 1.0)
    step_y[...] = plus - from_mask(window_at == lane_at - 1, 1.0)

    entries = center_ref.shape[1]
    gain = math.sqrt(0.5) / width_ref[...]
    level = jnp.log(peak_ref[...] * (1.0 / (depth_count * ranks)))
    tables[...] = jnp.zeros(tables.shape, jnp.float32)
    tables[0:1, 0:entries] = gain + gain
    tables[1:2, 0:entries] = gain * center_ref[...]
    tables[2:3, 0:entries] = level
    tables[3:6, 0:entries] = color_ref[...]

    load.wait()
    send_row.wait_send()
    send_col.wait_send()
    pltpu.make_async_remote_copy(
        src_ref=volume_ref.at[:, pl.ds(edge_row, ROWS), :],
        dst_ref=padded.at[:, pl.ds(got_row, ROWS), :],
        send_sem=halo_send.at[0],
        recv_sem=halo_recv.at[0],
        device_id=(me, row_partner),
        device_id_type=MESH,
    ).wait_recv()
    send_col.wait_recv()

    shade_x = 0.6 * math.sqrt(0.7)
    shade_y = 0.8 * math.sqrt(0.7)
    unit = math.gcd(piece, LANES)
    per_piece = piece // unit
    per_block = LANES // unit

    def post(segment, left):
        cols = pl.ds(left, span)
        slot = left // span
        there = lax.div(segment, per_piece)
        rows = pl.multiple_of(segment * unit, ROWS)
        inside = pl.multiple_of(lax.rem(segment, per_piece) * unit, ROWS)
        return pltpu.make_async_remote_copy(
            src_ref=outbox.at[:, pl.ds(rows, unit), cols],
            dst_ref=inbox.at[me, :, pl.ds(inside, unit), cols],
            send_sem=send_sem.at[segment, slot],
            recv_sem=recv_sem.at[me, lax.rem(segment, per_piece), slot],
            device_id=(there, tile),
            device_id_type=MESH,
        )

    blocks = height // LANES // 2
    transposed = (((1,), (1,)), ((), ()))

    def block(turn, carry):
        away = 1 - lax.div(turn, blocks)
        part = lax.rem(turn + me, blocks)
        area = lax.rem(side + away, 2)
        first = pl.multiple_of((area * blocks + part) * LANES, LANES)
        cells_half = span // CELL
        entry_rows = [jnp.broadcast_to(tables[p : p + 1, :], (cells_half, LANES)) for p in range(6)]

        def march(left):
            cols = pl.ds(left, span)
            first_cell = left // CELL

            def prepare(step, carry):
                index = index_ref[step, first_cell : first_cell + cells_half, pl.ds(first, LANES)]
                for p in range(6):
                    found = jnp.take_along_axis(entry_rows[p], index, axis=1, mode="promise_in_bounds")
                    begin = p * cells + first_cell
                    cell_params[step, begin : begin + cells_half, :] = found
                near = padded[step, pl.ds(pl.multiple_of(first + ROWS, ROWS), LANES), cols]
                above = padded[step, pl.ds(first, ROWS), cols]
                below = padded[step, pl.ds(pl.multiple_of(first + ROWS + LANES, ROWS), ROWS), cols]
                rows = jnp.concatenate([near, above, below], axis=0)
                flipped = lax.dot_general(half_eye[...], rows, transposed, preferred_element_type=jnp.float32)
                turned[step, RIM + left : RIM + left + span, :] = flipped[:, :LANES]
                grad_y[step, cols, :] = jnp.dot(
                    flipped.astype(jnp.bfloat16), step_y[...], preferred_element_type=jnp.float32
                )
                if left == 0:
                    rim = slab[step, pl.ds(first, LANES), :]
                    edges = lax.dot_general(rim_pick[...], rim, transposed, preferred_element_type=jnp.float32)
                    turned[step, 0:RIM, :] = edges[:RIM]
                    turned[step, RIM + width : 2 * RIM + width, :] = edges[RIM:]
                after = left + span
                if after < width:
                    beside = padded[
                        step, pl.ds(pl.multiple_of(first + ROWS, ROWS), LANES), after : after + LANES
                    ]
                    ahead = lax.dot_general(
                        half_eye[0:ROWS, 0:LANES], beside, transposed, preferred_element_type=jnp.float32
                    )
                    turned[step, RIM + after : 2 * RIM + after, :] = ahead[:RIM]
                return carry

            lax.fori_loop(0, depth_count, prepare, 0, unroll=4)

            def column(cell, carry):
                top = pl.multiple_of(cell * CELL, CELL)

                def sample(step, carry):
                    red, green, blue, trans = carry
                    value = turned[step, pl.ds(top + RIM, CELL), :]
                    gx = turned[step, pl.ds(top + RIM + 1, CELL), :] - turned[step, pl.ds(top + RIM - 1, CELL), :]
                    gy = grad_y[step, pl.ds(top, CELL), :]

                    def param(number):
                        row = cell_params[step, pl.ds(number * cells + cell, 1), :]
                        return jnp.broadcast_to(row, (CELL, LANES))

                    energy = gx * gx + gy * gy
                    facing = shade_x * gx + shade_y * gy
                    base = 1.0 + energy
                    rough = pl.reciprocal(base, approx=True)
                    shade = 0.3 + facing * facing * (rough * (2.0 - base * rough))
                    scaled = param(0) * value - param(1)
                    keep = jnp.exp(-(jnp.exp(param(2) - scaled * scaled) * energy))
                    weight = trans * (1.0 - keep) * shade
                    return (
                        red + weight * param(3),
                        green + weight * param(4),
                        blue + weight * param(5),
                        trans * keep,
                    )

                zero = jnp.zeros((CELL, LANES), jnp.float32)
                start = (zero, zero, zero, zero + 1.0)
                red, green, blue, trans = lax.fori_loop(0, depth_count, sample, start, unroll=True)
                for channel, image in enumerate((red, green, blue, 1.0 - trans)):
                    image_turned[channel, pl.ds(top, CELL), :] = image
                return carry

            lax.fori_loop(first_cell, first_cell + cells_half, column, 0)

            for channel in range(4):
                for at in range(left, left + span, LANES):
                    flat = image_turned[channel, at : at + LANES, :].T
                    outbox[channel, pl.ds(first, LANES), at : at + LANES] = encode(flat)

            def dispatch(number, carry):
                segment = (area * blocks + part) * per_block + number

                @pl.when(lax.div(segment, per_piece) != me)
                def _():
                    post(segment, left).start()

                return carry

            lax.fori_loop(0, per_block, dispatch, 0)

        for left in range(0, width, span):
            march(left)
        return carry

    lax.fori_loop(0, 2 * blocks, block, 0)
    mine = outbox.at[:, pl.ds(pl.multiple_of(me * piece, ROWS), piece), :]
    own = pltpu.make_async_copy(mine, inbox.at[me], own_sem)
    own.start()
    own.wait()

    def settle(number, carry):
        there = lax.rem(me + 1 + lax.div(number, per_piece), ranks)
        inside = lax.rem(number, per_piece)
        rows = pl.ds(pl.multiple_of(inside * unit, ROWS), unit)
        for left in range(0, width, span):
            post(there * per_piece + inside, left).wait_send()
            pltpu.make_async_remote_copy(
                src_ref=outbox.at[:, pl.ds(0, unit), pl.ds(left, span)],
                dst_ref=inbox.at[there, :, rows, pl.ds(left, span)],
                send_sem=send_sem.at[0, 0],
                recv_sem=recv_sem.at[there, inside, left // span],
                device_id=(there, tile),
                device_id_type=MESH,
            ).wait_recv()
        return carry

    lax.fori_loop(0, (ranks - 1) * per_piece, settle, 0)

    def merge(part, carry):
        rows = pl.ds(pl.multiple_of(part * ROWS, ROWS), ROWS)
        for left in range(0, width, span):
            cols = pl.ds(left, span)

            def layer(place, images):
                rank = order[place]
                clear = 1.0 - images[3]
                return tuple(images[c] + clear * decode(inbox[rank, c, rows, cols]) for c in range(4))

            zero = jnp.zeros((ROWS, span), jnp.float32)
            images = lax.fori_loop(0, ranks, layer, (zero,) * 4, unroll=True)
            for c in range(4):
                out_ref[c, rows, cols] = images[c]
        return carry

    lax.fori_loop(0, piece // ROWS, merge, 0)


def fused_device(ranks, tiles, volume, table_index, brick_position, tf_center, tf_width, tf_peak, tf_color):
    samples = volume[:, 0]
    index = jnp.swapaxes(table_index[:, 0], 1, 2)
    depth_count, height, width = samples.shape
    piece = height // ranks
    cells = index.shape[1]
    image = pl.pallas_call(
        functools.partial(march_kernel, ranks, tiles),
        out_shape=jax.ShapeDtypeStruct((4, piece, width), jnp.float32),
        in_specs=[
            pl.BlockSpec(memory_space=pltpu.SMEM),
            pl.BlockSpec(memory_space=pltpu.VMEM),
            pl.BlockSpec(memory_space=pltpu.VMEM),
            pl.BlockSpec(memory_space=pltpu.VMEM),
            pl.BlockSpec(memory_space=pltpu.VMEM),
            pl.BlockSpec(memory_space=pltpu.VMEM),
            pl.BlockSpec(memory_space=pl.ANY),
        ],
        out_specs=pl.BlockSpec(memory_space=pltpu.VMEM),
        scratch_shapes=[
            pltpu.VMEM((depth_count, height + 2 * ROWS, width), jnp.bfloat16),
            pltpu.VMEM((depth_count, height, LANES), jnp.bfloat16),
            pltpu.SMEM((ranks,), jnp.int32),
            pltpu.VMEM((2 * LANES, 2 * LANES), jnp.bfloat16),
            pltpu.VMEM((ROWS, LANES), jnp.bfloat16),
            pltpu.VMEM((LANES + 2 * ROWS, LANES), jnp.bfloat16),
            pltpu.VMEM((8, LANES), jnp.float32),
            pltpu.VMEM((depth_count, width + 2 * RIM, LANES), jnp.float32),
            pltpu.VMEM((depth_count, width, LANES), jnp.float32),
            pltpu.VMEM((depth_count, 6 * cells, LANES), jnp.float32),
            pltpu.VMEM((4, width, LANES), jnp.float32),
            pltpu.VMEM((4, height, width), jnp.int16),
            pltpu.VMEM((ranks, 4, piece, width), jnp.int16),
            pltpu.SemaphoreType.DMA,
            pltpu.SemaphoreType.DMA((2,)),
            pltpu.SemaphoreType.DMA((2,)),
            pltpu.SemaphoreType.DMA((height // math.gcd(piece, LANES), width // (2 * LANES))),
            pltpu.SemaphoreType.DMA((ranks, piece // math.gcd(piece, LANES), width // (2 * LANES))),
            pltpu.SemaphoreType.DMA,
        ],
        compiler_params=pltpu.CompilerParams(
            collective_id=0, has_side_effects=True, vmem_limit_bytes=56 * 1024 * 1024
        ),
    )(brick_position, tf_center[None], tf_width[None], tf_peak[None], tf_color, index, samples)
    return image[:, None]


def from_partner(value, axis, apart):
    return lax.ppermute(value, axis, [(i, i ^ 1 << apart) for i in range(lax.axis_size(axis))])


def light_sample(value, grad_x, grad_y, params, rgb, trans, inverse):
    energy = grad_x * grad_x + grad_y * grad_y
    facing = 0.6 * grad_x + 0.8 * grad_y
    shade = 0.3 + 0.7 * facing * facing / (1.0 + energy)
    scaled = (value - params[0]) / params[1]
    extinction = params[2] * jnp.exp(-0.5 * scaled * scaled) * energy * inverse
    keep = jnp.exp(-extinction)
    opacity = 1.0 - keep
    weight = trans * opacity
    rgb = rgb + weight[None] * params[3:6] * shade[None]
    trans = trans * keep
    return (rgb, trans)


def composite(layers):
    while layers.shape[1] > 1:
        front = layers[:, 0::2]
        back = layers[:, 1::2]
        layers = front + (1.0 - front[3:4]) * back
    return layers[:, 0]


def on_device(volume, table_index, brick_position, tf_center, tf_width, tf_peak, tf_color):
    tables = jnp.concatenate([tf_center[None], tf_width[None], tf_peak[None], tf_color], axis=0)
    samples = volume[:, 0]
    cells = table_index[:, 0]
    depth_count = samples.shape[0]
    height = samples.shape[1]
    width = samples.shape[2]
    cell_count = cells.shape[2]
    table_count = tables.shape[1]
    param_count = tables.shape[0]
    ranks = lax.axis_size("depth")
    inverse = 1.0 / (depth_count * ranks)
    tile_rank = lax.axis_index("tile")
    col_bit = tile_rank % 2
    row_bit = tile_rank // 2
    send_col = jnp.where(col_bit == 0, samples[:, :, width - 1], samples[:, :, 0])
    got_col = from_partner(send_col, "tile", 0)
    send_row = jnp.where(row_bit == 0, samples[:, height - 1, :], samples[:, 0, :])
    got_row = from_partner(send_row, "tile", 1)
    zero_col = jnp.zeros_like(got_col)
    zero_row = jnp.zeros_like(got_row)
    left_rim = jnp.where(col_bit == 1, got_col, zero_col)
    right_rim = jnp.where(col_bit == 0, got_col, zero_col)
    top_rim = jnp.where(row_bit == 1, got_row, zero_row)
    bottom_rim = jnp.where(row_bit == 0, got_row, zero_row)
    wide_pad = jnp.concatenate([left_rim[:, :, None], samples, right_rim[:, :, None]], axis=2)
    tall_pad = jnp.concatenate([top_rim[:, None, :], samples, bottom_rim[:, None, :]], axis=1)
    entries = jnp.arange(table_count, dtype=jnp.int32)
    table_grid = tables[:, :, None, None]

    def sample(step, carry):
        rgb, trans = carry
        wide = lax.dynamic_index_in_dim(wide_pad, step, 0, keepdims=False).astype(jnp.float32)
        tall = lax.dynamic_index_in_dim(tall_pad, step, 0, keepdims=False).astype(jnp.float32)
        cell_index = lax.dynamic_index_in_dim(cells, step, 0, keepdims=False)
        matches_cell = cell_index[None] == entries[:, None, None]
        cell_params = jnp.sum(jnp.where(matches_cell[None], table_grid, 0.0), axis=1)
        params = jnp.broadcast_to(cell_params[..., None], (param_count, height, cell_count, CELL))
        params = params.reshape(param_count, height, width)
        value = wide[:, 1:-1]
        grad_x = 0.5 * (wide[:, 2:] - wide[:, :-2])
        grad_y = 0.5 * (tall[2:, :] - tall[:-2, :])
        return light_sample(value, grad_x, grad_y, params, rgb, trans, inverse)

    start = (jnp.zeros((3, height, width), jnp.float32), jnp.ones((height, width), jnp.float32))
    rgb, trans = lax.fori_loop(0, depth_count, sample, start)
    partial_value = jnp.concatenate([rgb, (1.0 - trans)[None]], axis=0)
    piece_rows = height // ranks
    places = jnp.arange(ranks, dtype=jnp.int32)
    matches = brick_position[None, :] == places[:, None]
    rank_at = jnp.sum(jnp.where(matches, places[None, :], 0), axis=1)
    received = lax.all_to_all(partial_value, "depth", split_axis=1, concat_axis=0, tiled=True)
    stacked = received.reshape(ranks, 4, piece_rows, received.shape[2])
    ordered = jnp.take(stacked, rank_at, axis=0)
    image = composite(jnp.moveaxis(ordered, 0, 1))
    return image[:, None]


def fits(ranks, tiles, shape):
    height, width = shape[2], shape[3]
    even = ranks % 2 == 0 and tiles == 4 and height % ranks == 0
    return even and (height // ranks) % ROWS == 0 and width % (2 * LANES) == 0 and height % (2 * LANES) == 0


def solution(mesh):
    ranks = mesh.shape["depth"]
    tiles = mesh.shape["tile"]

    def program(volume, *rest):
        chosen = on_device
        if fits(ranks, tiles, volume.shape):
            chosen = functools.partial(fused_device, ranks, tiles)
        return jax.shard_map(
            chosen,
            mesh=mesh,
            in_specs=(P("depth", "tile", None, None), P("depth", "tile", None, None), P(), P(), P(), P(), P()),
            out_specs=P(None, "tile", "depth", None),
            check_vma=False,
        )(volume, *rest)

    return program
```
